512 devices in a mesh: face: 4 (over z_lo), tile: 64 (over y, z_hi, x), lev: 2 (over core).
Axes of the slice: x: 4, y: 4, z: 16 (z_hi: 4, z_lo: 4; z = z_hi * 4 + z_lo), core: 2. Of those that a mesh axis runs over, the one named last changes fastest.
Arguments:
- flux: float32 [2048, 8, 512], P(('face', 'tile')), may hold values from -6 to 6
- profile: float32 [16], P('lev'), may hold values from 0.2 to 1
- courant: float32 [2, 16, 512, 2048], P(None, 'lev', 'tile', 'face'), may hold values from 0.05 to 0.45
- winds: int32 [2, 16, 512, 2048], P(None, 'lev', 'tile', 'face'), may hold values from 0 to 1
- cells: int32 [64, 4, 128], P('tile', 'face'), may hold values from 0 to 4095, as said below
- counts: int32 [64, 4], P('tile', 'face'), may hold values from 32 to 128, as said below
- kernels: float32 [16, 64, 4, 128], P('lev', 'tile', 'face'), may hold values from 0.25 to 0.75
- month_weight: float32 [8, 64, 4, 128], P(None, 'tile', 'face'), may hold values from 0 to 1
- observed: float32 [64, 4, 128], P('tile', 'face'), may hold values from -8 to 8
- obs_weight: float32 [64, 4, 128], P('tile', 'face'), may hold values from 0.5 to 2
- precision: float32 [8], replicated, may hold values from 0.5 to 2
Outputs:
- flux_gradient: float32 [8, 512, 2048], P(None, 'tile', 'face')
- precision_gradient: float32 [8], replicated
The draws below stay inside these ranges and needn't reach their ends.
Inputs may be any that keep to these rules, and one draw needn't show every extreme that they name: Within each block the 128 entries are distinct cells, numbered row by row over the block's 8 rows of 512 cells; the first four slots of every block hold, in some order, a cell of the block's first column, one of its last column, and interior cells of its first row and of its last row. `counts`: slot s of a block holds a sounding when s is below the block's count; some block is full and some holds exactly 32.
All inputs are finite; a program needn't handle non-finite values.
Results may differ from the reference program's by a relative error of at most 0.00015.
Values sent between devices are 32-bit elements; how exact they have to be, the bound alone decides.
A program may use at most 64 MiB of HBM per device.

```python
import math
import jax
import jax.numpy as jnp
from jax import lax

NT = 8
RY = 8
SLOTS = 128
CX = 512
NL = 16
NYG = 512
NXG = 2048
N_FACE = 4
N_TILE = 64


def block_cells(block_key):
    keys = jax.random.split(block_key, 5)
    total = RY * CX
    west_cell = jax.random.randint(keys[1], (), 0, RY) * CX
    east_cell = jax.random.randint(keys[2], (), 0, RY) * CX + CX - 1
    south_cell = jax.random.randint(keys[3], (), 1, CX - 1)
    north_cell = (RY - 1) * CX + jax.random.randint(keys[4], (), 1, CX - 1)
    chosen = jnp.stack([west_cell, east_cell, south_cell, north_cell]).astype(jnp.int32)
    order_cells = jax.random.permutation(keys[0], total).astype(jnp.int32)
    marked = jnp.any(order_cells[:, None] == chosen[None, :], 1).astype(jnp.int32)
    ranking = jnp.argsort(1 - marked, stable=True)
    return order_cells[ranking][:SLOTS]


def draw_cells(key, part):
    key = jax.random.fold_in(key, 11)
    keys = jax.random.split(key, N_TILE * N_FACE)
    picks = jax.vmap(block_cells)(keys)
    return picks.reshape(N_TILE, N_FACE, SLOTS).astype(jnp.int32)


def draw_counts(key, part):
    key = jax.random.fold_in(key, 23)
    key_level, key_high, key_low = jax.random.split(key, 3)
    blocks = N_TILE * N_FACE
    level = jax.random.randint(key_level, (blocks,), 0, 16)
    least = SLOTS // 4
    loads = least + (SLOTS - least) * level * level // 225
    high = jax.random.randint(key_high, (), 0, blocks)
    low = (high + 1 + jax.random.randint(key_low, (), 0, blocks - 1)) % blocks
    loads = loads.at[high].set(SLOTS).at[low].set(least)
    return loads.reshape(N_TILE, N_FACE).astype(jnp.int32)


def touch_ends(values, key, smallest, largest):
    longest = values.shape.index(max(values.shape))
    spots = []
    for shift in (0, 1):
        where = [jax.random.randint(jax.random.fold_in(key, axis), (), 0, length) for axis, length in enumerate(values.shape)]
        where[longest] = (where[longest] + shift) % values.shape[longest]
        spots.append(tuple(where))
    return values.at[spots[0]].set(smallest).at[spots[1]].set(largest)


def block_levels(own_key, dims, cuts, smallest, largest):
    factor_of = 1.0
    for position, parts in cuts:
        draws = jax.random.uniform(jax.random.fold_in(jax.random.fold_in(own_key, 6), position), (parts,), jnp.float32, smallest / len(cuts), largest / len(cuts))
        factor_of = factor_of * jnp.repeat(jnp.exp(draws), dims[position] // parts).reshape((-1,) + (1,) * (len(dims) - 1 - position))
    return factor_of


def noise(key, shape, width, limit, pieces=(), held_as=jnp.bfloat16):
    values = width * jax.random.normal(key, shape, jnp.float32)
    if pieces:
        values = values * block_levels(key, shape, pieces, -0.22, 0.18)
    return jnp.clip(values, -limit, limit).astype(held_as)


def setup_inputs(seed: int = 0) -> dict:
    splits = jax.random.split(jax.random.key(seed), 12)
    return {
        "flux": noise(splits[0], (NXG, NT, NYG), 1.0, 6.0, ((0, 256),), jnp.float32),
        "profile": jnp.clip(jnp.exp(math.log(1.0) - 1.609438 * jax.random.uniform(splits[1], (NL,), jnp.float32) ** block_levels(splits[1], (NL,), ((0, 2),), -0.2, 0.2)), 0.2, 1.0),
        "courant": jnp.clip(0.05 + 0.39999999 * jax.random.uniform(splits[2], (2, NL, NYG, NXG), jnp.float32) ** block_levels(splits[2], (2, NL, NYG, NXG), ((1, 2), (2, 64), (3, 4)), -0.2, 0.2), 0.05, 0.45),
        "winds": touch_ends(jax.random.randint(splits[3], (2, NL, NYG, NXG), 0, 2), jax.random.fold_in(splits[3], 1), 0, 1).astype(jnp.int32),
        "cells": draw_cells(jax.random.fold_in(splits[11], 71), 0),
        "counts": draw_counts(jax.random.fold_in(splits[11], 71), 0),
        "kernels": jnp.clip(0.25 + 0.5 * jax.random.uniform(splits[6], (NL, N_TILE, N_FACE, SLOTS), jnp.float32) ** block_levels(splits[6], (NL, N_TILE, N_FACE, SLOTS), ((0, 2), (1, 64), (2, 4)), -0.2, 0.2), 0.25, 0.75),
        "month_weight": jnp.clip(1.0 * jax.random.uniform(splits[7], (NT, N_TILE, N_FACE, SLOTS), jnp.float32) ** block_levels(splits[7], (NT, N_TILE, N_FACE, SLOTS), ((1, 64), (2, 4)), -0.2, 0.2), 0.0, 1.0),
        "observed": noise(splits[8], (N_TILE, N_FACE, SLOTS), 2.0, 8.0, ((0, 64), (1, 4)), jnp.float32),
        "obs_weight": jnp.clip(jnp.exp(math.log(2.0) - 1.3862944 * jax.random.uniform(splits[9], (N_TILE, N_FACE, SLOTS), jnp.float32) ** block_levels(splits[9], (N_TILE, N_FACE, SLOTS), ((0, 64), (1, 4)), -0.2, 0.2)), 0.5, 2.0),
        "precision": jnp.clip(jnp.exp(jax.random.uniform(splits[10], (NT,), jnp.float32, math.log(0.5), math.log(2.0))), 0.5, 2.0),
    }


KAPPA = 0.025


def coefficients(courant, winds):
    east_flag = (winds[0] == 1).astype(jnp.float32)
    north_flag = (winds[1] == 1).astype(jnp.float32)
    w_west = courant[0] * (1.0 - east_flag) + KAPPA
    w_east = courant[0] * east_flag + KAPPA
    w_south = courant[1] * (1.0 - north_flag) + KAPPA
    w_north = courant[1] * north_flag + KAPPA
    w_centre = 1.0 - courant[0] - courant[1] - 4.0 * KAPPA
    return w_centre, w_west, w_east, w_south, w_north


def rows_below(field):
    zero = jnp.zeros_like(field[:, :1])
    return jnp.concatenate([zero, field[:, :-1]], 1)


def rows_above(field):
    zero = jnp.zeros_like(field[:, :1])
    return jnp.concatenate([field[:, 1:], zero], 1)


def forward(conc, coeffs):
    w_centre, w_west, w_east, w_south, w_north = coeffs
    return (w_centre * conc + w_west * jnp.roll(conc, 1, 2) + w_east * jnp.roll(conc, -1, 2)
            + w_south * rows_below(conc) + w_north * rows_above(conc))


def backward(grad, coeffs):
    w_centre, w_west, w_east, w_south, w_north = coeffs
    return (w_centre * grad + jnp.roll(w_west * grad, -1, 2) + jnp.roll(w_east * grad, 1, 2)
            + rows_above(w_south * grad) + rows_below(w_north * grad))


def reference(flux, profile, courant, winds, cells, counts, kernels, month_weight, observed, obs_weight, precision):
    flux_field = jnp.transpose(flux, (1, 2, 0))
    coeffs = coefficients(courant, winds)
    block_row = jnp.arange(N_TILE, dtype=jnp.int32)[:, None, None] * RY + cells // CX
    block_col = jnp.arange(N_FACE, dtype=jnp.int32)[None, :, None] * CX + cells % CX
    index = (block_row * NXG + block_col).reshape(-1).astype(jnp.int32)
    valid = (jnp.arange(SLOTS, dtype=jnp.int32)[None, None, :] < counts[:, :, None]).reshape(-1)
    kern = kernels.reshape(NL, -1)
    monthly = month_weight.reshape(NT, -1)

    def sample(surface):
        conc = profile[:, None, None] * surface[None]
        conc = forward(forward(conc, coeffs), coeffs)
        return conc.reshape(NL, -1)[:, index]

    sampled = lax.map(sample, flux_field)
    model = jnp.sum(kern * jnp.sum(monthly[:, None, :] * sampled, 0), 0)
    forcing = jnp.where(valid, obs_weight.reshape(-1) * (observed.reshape(-1) - model), 0.0)

    def back(weight_row):
        values = kern * (weight_row * forcing)[None]
        lam = jnp.zeros((NL, NYG * NXG), jnp.float32).at[:, index].add(values).reshape(NL, NYG, NXG)
        lam = backward(backward(lam, coeffs), coeffs)
        return jnp.sum(profile[:, None, None] * lam, 0)

    adj = lax.map(back, monthly)
    flux_gradient = precision[:, None, None] * flux_field - adj
    mean_square = jnp.sum(adj * adj, axis=(1, 2)) / (NYG * NXG)
    precision_gradient = 0.5 / precision - 0.5 * mean_square / (precision * precision)
    return flux_gradient, precision_gradient
```

```python
import functools

import jax
import jax.numpy as jnp
from jax import lax
from jax.experimental import pallas as pl
from jax.experimental.pallas import tpu as pltpu
from jax.sharding import PartitionSpec as P

KAPPA = 0.025
MESH = pl.DeviceIdType.MESH
F32 = jnp.float32
BF16 = jnp.bfloat16

NT, NLEV, ROWS, COLS, SLOTS = 8, 8, 8, 512, 128
WIDE = COLS + 128
STEPS = ((0, 0), (0, -1), (0, 1), (-1, 0), (1, 0))
OFFSETS = tuple((dy, dx) for dy in range(-2, 3) for dx in range(-2, 3) if abs(dy) + abs(dx) <= 2)
N_OFF = len(OFFSETS)
PLANES = 24


def iota(shape, dim):
    return lax.broadcasted_iota(jnp.int32, shape, dim)


def lroll(x, by):
    by = by % x.shape[-1]
    return x if by == 0 else pltpu.roll(x, by, x.ndim - 1)


def rshift(own, halo, by):
    if by == 0:
        return own, halo
    axis = own.ndim - 2
    turned_own = pltpu.roll(own, by % ROWS, axis)
    turned_halo = pltpu.roll(halo, by % ROWS, axis)
    sub = iota(own.shape, axis)
    cross = sub < by if by > 0 else sub >= ROWS + by
    return jnp.where(cross, turned_halo, turned_own), jnp.where(cross, turned_own, turned_halo)


def exact_dot(values, onehot, dims):
    high = values.astype(BF16)
    rest = values - high.astype(F32)
    middle = rest.astype(BF16)
    low = (rest - middle.astype(F32)).astype(BF16)
    dot = lambda part: lax.dot_general(part, onehot, (dims, ((), ())), preferred_element_type=F32)
    return dot(high) + (dot(middle) + dot(low))


def remote(src, dst, send, recv, device):
    return pltpu.make_async_remote_copy(
        src_ref=src, dst_ref=dst, send_sem=send, recv_sem=recv, device_id=device, device_id_type=MESH
    )


def main_kernel(
    flux_h, cour_h, wind_h, prof, cells, counts, kern, month, observed, obs_w, prec,
    fg_out, sq_out,
    flux_v, cour_v, wind_v, w_own, w_halo, w_edge, col_s, col_r,
    s_buf, i_buf, z_buf, r_buf, h_buf, f_buf,
    l_buf, slot_v, nb, dense, m_sh, a_sh, fg_v, az, ap,
    loc_sem, coef_s, coef_r, st1_s, st1_r, st2_s, st2_r, hal_s, hal_r, fx_s, fx_r,
    lev_s, lev_r, nb_s, nb_r, az_s, az_r, ap_s, ap_r,
):
    face, tile, lev = lax.axis_index("face"), lax.axis_index("tile"), lax.axis_index("lev")
    ty, tz, tx = tile // 16, (tile // 4) % 4, tile % 4
    z, plane = tz * 4 + face, ty * 4 + tx

    def in_plane(k):
        other = lax.rem(plane + k, 16)
        return other, (face, (other // 4) * 16 + tz * 4 + other % 4, lev)

    def in_line(k):
        other = lax.rem(z + k, 16)
        return (other % 4, ty * 16 + (other // 4) * 4 + tx, lev)

    def near(df, dt):
        return (lax.rem(face + 4 + df, 4), lax.rem(tile + 64 + dt, 64), lev)

    peer = (face, tile, 1 - lev)
    sends = ((0, -1), (0, 1), (-1, 0), (1, 0), (-1, -1), (1, -1), (-1, 1), (1, 1))

    bar = pltpu.get_barrier_semaphore()
    greet = [peer] + [in_line(k) for k in range(1, 16)] + [in_plane(k)[1] for k in range(1, 16)]
    greet += [near(*d) for d in sends if d[1] != 0]
    for device in greet:
        pl.semaphore_signal(bar, inc=1, device_id=device, device_id_type=MESH)

    local = [
        pltpu.make_async_copy(flux_h, flux_v, loc_sem.at[0]),
        pltpu.make_async_copy(cour_h, cour_v, loc_sem.at[1]),
        pltpu.make_async_copy(wind_h, wind_v, loc_sem.at[2]),
    ]
    for copy in local:
        copy.start()

    local[0].wait()
    by_tracer = jnp.swapaxes(flux_v[...], 0, 1).reshape(NT * 8, 512)
    turned = jnp.transpose(jnp.concatenate([by_tracer, by_tracer], axis=0)).reshape(64, 8, 128)
    nothing = jnp.zeros((1, 8, 128), F32)
    above = jnp.concatenate([turned[1:], nothing], axis=0)
    below = jnp.concatenate([nothing, turned[:-1]], axis=0)
    around = jnp.where(iota((64, 8, 128), 1) < 4, above, below)
    half = jnp.where(lev == 0, turned, around).reshape(4, 2, 2, 4, 8, 128)
    blocks = jnp.where(iota((4, 2, 4, 8, 128), 4) < 64, half[:, :, 0], half[:, :, 1])
    for y in range(4):
        for x in range(4):
            s_buf[y * 4 + x] = blocks[y, :, x]

    local[1].wait()
    local[2].wait()
    u, v = cour_v[0], cour_v[1]
    east, north = wind_v[0] == 1, wind_v[1] == 1
    w_own[1, :, :, :COLS] = jnp.where(east, 0.0, u) + KAPPA
    w_own[2, :, :, :COLS] = jnp.where(east, u, 0.0) + KAPPA
    w_own[3, :, :, :COLS] = jnp.where(north, 0.0, v) + KAPPA
    w_own[4, :, :, :COLS] = jnp.where(north, v, 0.0) + KAPPA
    w_own[0, :, :, :COLS] = 1.0 - u - v - 4.0 * KAPPA
    lane = iota((ROWS, 128), 1)
    last, first = jnp.zeros((ROWS, 128), F32), jnp.zeros((ROWS, 128), F32)
    for e in range(4):
        for l in range(NLEV):
            k = e * NLEV + l
            last = jnp.where(lane == k, lroll(w_own[1 + e, l, :, COLS - 128 : COLS], k - 127), last)
            first = jnp.where(lane == k, lroll(w_own[1 + e, l, :, :128], k), first)
    col_s[0] = last
    col_s[1] = first

    pl.semaphore_wait(bar, len(greet))

    stage1 = []
    for k in range(1, 16):
        other, device = in_plane(k)
        copy = remote(s_buf.at[other], i_buf.at[plane], st1_s.at[k], st1_r.at[k], device)
        copy.start()
        stage1.append(copy)
    coef = [
        remote(w_own.at[pl.ds(1, 4), :, pl.ds(7, 1), pl.ds(0, COLS)], w_edge.at[:, :, pl.ds(7, 1), :], coef_s.at[0], coef_r.at[0], near(0, 1)),
        remote(w_own.at[pl.ds(1, 4), :, pl.ds(0, 1), pl.ds(0, COLS)], w_edge.at[:, :, pl.ds(0, 1), :], coef_s.at[1], coef_r.at[1], near(0, -1)),
        remote(col_s.at[0], col_r.at[0], coef_s.at[2], coef_r.at[2], near(1, 0)),
        remote(col_s.at[1], col_r.at[1], coef_s.at[3], coef_r.at[3], near(-1, 0)),
    ]
    for copy in coef:
        copy.start()
    i_buf[plane] = s_buf[plane]

    slot = iota((1, SLOTS), 1)
    cell = cells[0].astype(F32)
    row = jnp.floor(cell * (1.0 / COLS))
    col = cell - COLS * row
    sub = iota((ROWS, SLOTS), 0).astype(F32)
    row_mask = jnp.where(sub == row, 1.0, 0.0)
    onehot = jnp.where(iota((COLS, SLOTS), 0).astype(F32) == col, 1.0, 0.0).astype(BF16)
    weight = jnp.where(slot < counts[0, 0], obs_w[0], 0.0)
    kern_rows = (kern[:, 0, 0, :][:, None, :] * row_mask[None]).reshape(NLEV * ROWS, SLOTS)
    kern_dense = exact_dot(kern_rows, onehot, ((1,), (1,))).reshape(NLEV, ROWS, COLS)
    level = iota((NLEV, ROWS, COLS), 0)
    prof_dense = jnp.zeros((NLEV, ROWS, COLS), F32)
    for l in range(NLEV):
        prof_dense = jnp.where(level == l, prof[l], prof_dense)
    kp = kern_dense * prof_dense

    for copy in stage1:
        copy.wait()
    lane6 = iota((2, 4, 8, 128), 3)
    for hi in range(2):
        low_y, high_y = i_buf_view(i_buf, hi)
        z_buf[2 * hi] = jnp.where(lane6 < 64, low_y, lroll(high_y, 64))
        z_buf[2 * hi + 1] = jnp.where(lane6 < 64, lroll(low_y, 64), high_y)
    stage2 = []
    for k in range(1, 4):
        to = lax.rem(tz + k, 4)
        copy = remote(z_buf.at[to], r_buf.at[tz], st2_s.at[k], st2_r.at[k], (face, ty * 16 + to * 4 + tx, lev))
        copy.start()
        stage2.append(copy)

    def halo_copy(side, to):
        there = lax.rem(face + (3 if side == 0 else 1), 4)
        src = (0, 0) if side == 0 else (1, 3)
        device = (there, ty * 16 + to * 4 + tx, lev)
        return remote(z_buf.at[(to, *src)], h_buf.at[side], hal_s.at[side, to], hal_r.at[side], device)

    @pl.when(tz == 0)
    def _():
        for to in range(4):
            halo_copy(0, to).start()

    @pl.when(tz == 3)
    def _():
        for to in range(4):
            halo_copy(1, to).start()

    r_buf[tz] = z_buf[tz]

    for copy in coef:
        copy.wait()
    right, left = col_r[1], col_r[0]
    for e in range(4):
        for l in range(NLEV):
            k = e * NLEV + l
            w_own[1 + e, l, :, COLS:] = jnp.where(
                lane == 0, lroll(right, -k), jnp.where(lane == 127, lroll(left, 127 - k), 0.0)
            )
    w_own[0, :, :, COLS:] = 1.0 - (
        w_own[1, :, :, COLS:] + w_own[2, :, :, COLS:] + w_own[3, :, :, COLS:] + w_own[4, :, :, COLS:]
    )
    sub4 = iota((4, NLEV, ROWS, COLS), 2)
    there = ((sub4 == 0) & (tile < 63)) | ((sub4 == 7) & (tile > 0))
    edges = jnp.where(there, w_edge[...], 0.0)
    w_halo[1:] = edges
    sub3 = iota((NLEV, ROWS, COLS), 1)
    there = ((sub3 == 0) & (tile < 63)) | ((sub3 == 7) & (tile > 0))
    w_halo[0] = jnp.where(there, 1.0 - (edges[0] + edges[1] + edges[2] + edges[3]), 0.0)

    stencil = {}

    def add(offset, term):
        stencil[offset] = stencil[offset] + term if offset in stencil else term

    for e1, (dy, dx) in enumerate(STEPS):
        g = kp * w_own[e1, :, :, :COLS]
        for e2, (ey, ex) in enumerate(STEPS):
            offset = (dy + ey, dx + ex)
            if dy == 0 and dx == 0:
                add(offset, jnp.sum(g * w_own[e2, :, :, :COLS], axis=0))
            elif dy == 0:
                h = lroll(jnp.concatenate([g, jnp.zeros((NLEV, ROWS, 128), F32)], axis=-1), dx)
                add(offset, lroll(jnp.sum(h * w_own[e2], axis=0), -dx)[:, :COLS])
            else:
                h, h_halo = rshift(g, jnp.zeros_like(g), dy)
                p, p_halo = jnp.sum(h * w_own[e2, :, :, :COLS], axis=0), jnp.sum(h_halo * w_halo[e2], axis=0)
                add(offset, rshift(p, p_halo, -dy)[0])
    spread = jnp.concatenate([stencil[o] for o in OFFSETS] + [jnp.zeros((3 * ROWS, COLS), F32)], axis=0)
    picked = exact_dot(spread, onehot, ((1,), (0,))).reshape(16, ROWS, SLOTS)
    l_buf[0] = jnp.sum(picked * row_mask[None], axis=1)
    to_peer = remote(l_buf.at[0], l_buf.at[1], lev_s, lev_r, peer)
    to_peer.start()
    to_peer.wait()

    sub16 = iota((16, SLOTS), 0)
    table = l_buf[0] + l_buf[1]
    table = jnp.where(sub16 == 13, observed[0], table)
    table = jnp.where(sub16 == 14, weight, table)
    slot_v[8:24] = jnp.where(sub16 == 15, cell, table)
    slot_v[0:8] = month[:, 0, 0, :]
    around_copies = []
    for k, d in enumerate(sends):
        copy = remote(slot_v, nb.at[k], nb_s.at[k], nb_r.at[k], near(*d))
        copy.start()
        around_copies.append(copy)

    def rows_of(values, mask):
        return (values[:, None, :] * mask[None]).reshape(PLANES * ROWS, SLOTS)

    own = exact_dot(rows_of(slot_v[...], row_mask), onehot, ((1,), (1,)))
    dense[0, :, :, :COLS] = own.reshape(PLANES, ROWS, COLS)

    for copy in around_copies:
        copy.wait()
    up, down = tile < 63, tile > 0

    def place(k):
        c = nb[k, 23:24, :]
        r = jnp.floor(c * (1.0 / COLS))
        return r, c - COLS * r

    def near_rows(r, upper):
        keep = (r <= 1.0) & up if upper else (r >= 6.0) & down
        return jnp.where((sub == r) & keep, 1.0, 0.0)

    def near_cols(c, righter):
        target = iota((128, SLOTS), 0).astype(F32)
        hit = (target == c) & (c <= 1.0) if righter else (target == c - (COLS - 128.0)) & (c >= COLS - 2.0)
        return jnp.where(hit, 1.0, 0.0).astype(BF16)

    values, hots = [], []
    for k, upper in ((0, True), (1, False)):
        r, c = place(k)
        values.append(rows_of(nb[k], near_rows(r, upper)))
        hots.append(jnp.where(iota((COLS, SLOTS), 0).astype(F32) == c, 1.0, 0.0).astype(BF16))
    out = exact_dot(jnp.concatenate(values, axis=1), jnp.concatenate(hots, axis=1), ((1,), (1,)))
    dense[1, :, :, :COLS] = out.reshape(PLANES, ROWS, COLS)
    values, hots = [], []
    for k, righter in ((2, True), (3, False)):
        r, c = place(k)
        values.append(rows_of(nb[k], jnp.where(sub == r, 1.0, 0.0)))
        hots.append(near_cols(c, righter))
    out = exact_dot(jnp.concatenate(values, axis=1), jnp.concatenate(hots, axis=1), ((1,), (1,)))
    dense[0, :, :, COLS:] = out.reshape(PLANES, ROWS, 128)
    values, hots = [], []
    for k, upper, righter in ((4, True, True), (5, True, False), (6, False, True), (7, False, False)):
        r, c = place(k)
        values.append(rows_of(nb[k], near_rows(r, upper)))
        hots.append(near_cols(c, righter))
    out = exact_dot(jnp.concatenate(values, axis=1), jnp.concatenate(hots, axis=1), ((1,), (1,)))
    dense[1, :, :, COLS:] = out.reshape(PLANES, ROWS, 128)

    for dx in range(-2, 3):
        months = lroll(dense[0, 0:8], dx), lroll(dense[1, 0:8], dx)
        for i, (oy, ox) in enumerate(OFFSETS):
            if ox == dx:
                m_own, m_halo = rshift(*months, oy)
                m_sh[i, 0] = m_own
                m_sh[i, 1] = m_halo
                a_own, a_halo = rshift(lroll(dense[0, 8 + i], dx), lroll(dense[1, 8 + i], dx), oy)
                a_sh[i, 0] = a_own
                a_sh[i, 1] = a_halo

    for copy in stage2:
        copy.wait()

    @pl.when(tz == 0)
    def _():
        for to in range(4):
            halo_copy(0, to).wait_send()

    @pl.when(tz == 3)
    def _():
        for to in range(4):
            halo_copy(1, to).wait_send()

    for side in range(2):
        halo_copy(side, 0).wait_recv()
    parts = [r_buf[i // 4, :, i % 4] for i in range(16)]
    lanes = iota((2, 8, 128), 2)
    for step in (1, 2, 4, 8):
        upper_half = (lanes // (8 * step)) % 2 == 1
        for i in range(16):
            if i & step == 0:
                a, b = parts[i], parts[i + step]
                parts[i] = jnp.where(upper_half, lroll(b, 8 * step), a)
                parts[i + step] = jnp.where(upper_half, b, lroll(a, -8 * step))
    for g in range(16):
        for y in range(2):
            f_buf[lev, g % 8, :, (2 * y + g // 8) * 128 : (2 * y + g // 8 + 1) * 128] = parts[g][y]
    for t in range(NT):
        f_buf[lev, t, :, COLS:] = jnp.where(
            lane < 4, lroll(h_buf[0], -8 * t), jnp.where(lane >= 124, lroll(h_buf[1], 56 - 8 * t), 0.0)
        )
    swap = remote(f_buf.at[lev], f_buf.at[lev], fx_s, fx_r, peer)
    swap.start()
    swap.wait()

    by_row = {}
    for i, (dy, dx) in enumerate(OFFSETS):
        pair = tuple(lroll(a_sh[i, h] * jnp.sum(m_sh[i, h] * f_buf[h], axis=0), -dx) for h in range(2))
        by_row[dy] = tuple(p + q for p, q in zip(by_row[dy], pair)) if dy in by_row else pair
    model = None
    for dy, pair in by_row.items():
        pair = rshift(*pair, -dy)
        model = pair if model is None else tuple(p + q for p, q in zip(model, pair))
    forcing = tuple(dense[h, 22] * (dense[h, 21] - model[h]) for h in range(2))
    adj = jnp.zeros((NT, ROWS, COLS), F32)
    for dx in range(-2, 3):
        moved = tuple(lroll(f, dx) for f in forcing)
        for i, (oy, ox) in enumerate(OFFSETS):
            if ox == dx:
                q = (a_sh[i, 0] * rshift(*moved, oy)[0])[:, :COLS]
                adj = adj + q[None] * m_sh[i, 0, :, :, :COLS]

    square = adj * adj
    square = square[..., :128] + square[..., 128:256] + square[..., 256:384] + square[..., 384:]
    square = jnp.sum(square, axis=1)
    for by in (64, 32, 16):
        square = square + lroll(square, by)
    mine = jnp.where(lane // 16 == iota((ROWS, 128), 0), square, 0.0)
    az[z] = jnp.broadcast_to(jnp.sum(mine, axis=0, keepdims=True), (8, 128))
    copies = []
    for k in range(1, 16):
        copy = remote(az.at[z, pl.ds(0, 1)], az.at[z, pl.ds(0, 1)], az_s.at[k], az_r.at[k], in_line(k))
        copy.start()
        copies.append(copy)
    for t in range(NT):
        fg_v[t] = prec[t] * f_buf[0, t, :, :COLS] - adj[t]
    out_copy = pltpu.make_async_copy(fg_v, fg_out, loc_sem.at[3])
    out_copy.start()
    for copy in copies:
        copy.wait()
    total = az[0, 0:1]
    for i in range(1, 16):
        total = total + az[i, 0:1]
    ap[plane] = jnp.broadcast_to(total, (8, 128))
    copies = []
    for k in range(1, 16):
        copy = remote(ap.at[plane, pl.ds(0, 1)], ap.at[plane, pl.ds(0, 1)], ap_s.at[k], ap_r.at[k], in_plane(k)[1])
        copy.start()
        copies.append(copy)
    for copy in copies:
        copy.wait()
    total = ap[0, 0:1]
    for i in range(1, 16):
        total = total + ap[i, 0:1]
    sq_out[...] = jnp.broadcast_to(total, (8, 128))
    out_copy.wait()


def i_buf_view(i_buf, hi):
    low = jnp.concatenate([i_buf[0:4, hi][None], i_buf[8:12, hi][None]], axis=0)
    high = jnp.concatenate([i_buf[4:8, hi][None], i_buf[12:16, hi][None]], axis=0)
    return low, high


def last_kernel(all_cells, fg_in, sq, prec, fg_out, pg_out, sem):
    copy = pltpu.make_async_copy(fg_in, fg_out, sem)
    copy.start()
    lane, sub = iota((8, 128), 1), iota((8, 128), 0)
    sums = jnp.sum(jnp.where(lane // 16 == sub, sq[...], 0.0), axis=1, keepdims=True)
    row = jnp.sum(jnp.where(lane == sub, sums, 0.0), axis=0, keepdims=True)[:, :8]
    p = prec[...].reshape(1, 8)
    pg_out[...] = (0.5 / p - 0.5 * (row / all_cells) / (p * p)).reshape(8)
    copy.wait()


def on_device(flux, profile, courant, winds, cells, counts, kernels, month_weight, observed, obs_weight, precision):
    vmem = pl.BlockSpec(memory_space=pltpu.VMEM)
    smem = pl.BlockSpec(memory_space=pltpu.SMEM)
    hbm = pl.BlockSpec(memory_space=pl.ANY)
    dma = pltpu.SemaphoreType.DMA

    def buf(*shape, dtype=F32):
        return pltpu.VMEM(shape, dtype)

    fg, sq = pl.pallas_call(
        main_kernel,
        name="gradient",
        out_shape=(jax.ShapeDtypeStruct((NT, ROWS, COLS), F32), jax.ShapeDtypeStruct((8, 128), F32)),
        in_specs=[hbm, hbm, hbm, smem, vmem, smem, vmem, vmem, vmem, vmem, smem],
        out_specs=(hbm, vmem),
        scratch_shapes=[
            buf(8, NT, 512), buf(2, NLEV, ROWS, COLS), buf(2, NLEV, ROWS, COLS, dtype=jnp.int32),
            buf(5, NLEV, ROWS, WIDE), buf(5, NLEV, ROWS, COLS), buf(4, NLEV, ROWS, COLS), buf(2, 8, 128), buf(2, 8, 128),
            buf(16, 2, 8, 128), buf(16, 2, 8, 128), buf(4, 2, 4, 8, 128), buf(4, 2, 4, 8, 128), buf(2, 8, 128),
            buf(2, NT, ROWS, WIDE),
            buf(2, 16, SLOTS), buf(PLANES, SLOTS), buf(8, PLANES, SLOTS), buf(2, PLANES, ROWS, WIDE),
            buf(N_OFF, 2, NT, ROWS, WIDE), buf(N_OFF, 2, ROWS, WIDE), buf(NT, ROWS, COLS), buf(16, 8, 128), buf(16, 8, 128),
            dma((4,)), dma((4,)), dma((4,)), dma((16,)), dma((16,)), dma((4,)), dma((4,)), dma((2, 4)), dma((2,)), dma, dma,
            dma, dma, dma((8,)), dma((8,)), dma((16,)), dma((16,)), dma((16,)), dma((16,)),
        ],
        compiler_params=pltpu.CompilerParams(collective_id=0, has_side_effects=True, vmem_limit_bytes=48 * 2**20),
    )(flux, courant, winds, profile, cells, counts, kernels, month_weight, observed, obs_weight, precision)
    all_cells = float(ROWS * COLS * lax.axis_size("tile") * lax.axis_size("face"))
    return pl.pallas_call(
        functools.partial(last_kernel, all_cells),
        name="finish",
        out_shape=(jax.ShapeDtypeStruct((NT, ROWS, COLS), F32), jax.ShapeDtypeStruct((8,), F32)),
        in_specs=[hbm, vmem, vmem],
        out_specs=(hbm, vmem),
        scratch_shapes=[dma],
    )(fg, sq, precision)


def solution(mesh):
    return jax.shard_map(
        on_device,
        mesh=mesh,
        in_specs=(
            P(("face", "tile"), None, None),
            P("lev"),
            P(None, "lev", "tile", "face"),
            P(None, "lev", "tile", "face"),
            P("tile", "face", None),
            P("tile", "face"),
            P("lev", "tile", "face", None),
            P(None, "tile", "face", None),
            P("tile", "face", None),
            P("tile", "face", None),
            P(),
        ),
        out_specs=(P(None, "tile", "face"), P()),
        check_vma=False,
    )
```

```python
import functools

import jax
import jax.numpy as jnp
from jax import lax
from jax.experimental import pallas as pl
from jax.experimental.pallas import tpu as pltpu
from jax.sharding import PartitionSpec as P

KAPPA = 0.025
MESH = pl.DeviceIdType.MESH
F32 = jnp.float32
BF16 = jnp.bfloat16

NT, NLEV, ROWS, COLS, SLOTS = 8, 8, 8, 512, 128
WIDE = COLS + 128
STEPS = ((0, 0), (0, -1), (0, 1), (-1, 0), (1, 0))
OFFSETS = tuple((dy, dx) for dy in range(-2, 3) for dx in range(-2, 3) if abs(dy) + abs(dx) <= 2)
N_OFF = len(OFFSETS)
PLANES = 24


def iota(shape, dim):
    return lax.broadcasted_iota(jnp.int32, shape, dim)


def lroll(x, by):
    by = by % x.shape[-1]
    return x if by == 0 else pltpu.roll(x, by, x.ndim - 1)


def rshift(own, halo, by):
    if by == 0:
        return own, halo
    axis = own.ndim - 2
    turned_own = pltpu.roll(own, by % ROWS, axis)
    turned_halo = pltpu.roll(halo, by % ROWS, axis)
    sub = iota(own.shape, axis)
    cross = sub < by if by > 0 else sub >= ROWS + by
    return jnp.where(cross, turned_halo, turned_own), jnp.where(cross, turned_own, turned_halo)


def exact_dot(values, onehot, dims):
    high = values.astype(BF16)
    rest = values - high.astype(F32)
    middle = rest.astype(BF16)
    low = (rest - middle.astype(F32)).astype(BF16)
    dot = lambda part: lax.dot_general(part, onehot, (dims, ((), ())), preferred_element_type=F32)
    return dot(high) + (dot(middle) + dot(low))


def remote(src, dst, send, recv, device):
    return pltpu.make_async_remote_copy(
        src_ref=src, dst_ref=dst, send_sem=send, recv_sem=recv, device_id=device, device_id_type=MESH
    )


def main_kernel(
    all_cells,
    flux_h, prof_h, cour_h, wind_h, cells_h, kern_h, month_h, observed_h, obs_w_h, prec_h, counts,
    fg_out, pg_out,
    prof, cells, kern, month, observed, obs_w, prec, prec_v,
    flux_v, cour_v, wind_v, w_own, w_halo, row_s, row_r, col_s, col_r,
    s_buf, i_buf, z_buf, r_buf, h_buf, f_buf,
    l_buf, slot_v, nb, corner_s, corner_r, dense, m_sh, a_sh, az, ap,
    loc_sem, coef_s, coef_r, st1_s, st1_r, st2_s, st2_r, hal_s, hal_r, fx_s, fx_r,
    lev_s, lev_r, nb_s, nb_r, az_s, az_r, ap_s, ap_r,
):
    face, tile, lev = lax.axis_index("face"), lax.axis_index("tile"), lax.axis_index("lev")
    ty, tz, tx = tile // 16, (tile // 4) % 4, tile % 4
    z, plane = tz * 4 + face, ty * 4 + tx

    def in_plane(k):
        other = lax.rem(plane + k, 16)
        return other, (face, (other // 4) * 16 + tz * 4 + other % 4, lev)

    def in_line(k):
        other = lax.rem(z + k, 16)
        return (other % 4, ty * 16 + (other // 4) * 4 + tx, lev)

    def near(df, dt):
        return (lax.rem(face + 4 + df, 4), lax.rem(tile + 64 + dt, 64), lev)

    peer = (face, tile, 1 - lev)
    sends = ((0, -1), (0, 1), (-1, 0), (1, 0), (-1, -1), (1, -1), (-1, 1), (1, 1))

    bar = pltpu.get_barrier_semaphore()
    greet = [peer] + [in_line(k) for k in range(1, 16)] + [in_plane(k)[1] for k in range(1, 16)]
    greet += [near(*d) for d in sends if d[1] != 0]
    for device in greet:
        pl.semaphore_signal(bar, inc=1, device_id=device, device_id_type=MESH)

    local = [
        pltpu.make_async_copy(src, dst, loc_sem.at[i])
        for i, (src, dst) in enumerate(
            (
                (flux_h, flux_v), (cour_h, cour_v), (wind_h, wind_v), (cells_h, cells), (kern_h, kern),
                (prof_h, prof), (obs_w_h, obs_w), (observed_h, observed), (month_h, month), (prec_h, prec), (prec_h, prec_v),
            )
        )
    ]
    for copy in local:
        copy.start()

    local[0].wait()
    by_tracer = jnp.swapaxes(flux_v[...], 0, 1).reshape(NT * 8, 512)
    turned = jnp.transpose(jnp.concatenate([by_tracer, by_tracer], axis=0)).reshape(64, 8, 128)
    nothing = jnp.zeros((1, 8, 128), F32)
    above = jnp.concatenate([turned[1:], nothing], axis=0)
    below = jnp.concatenate([nothing, turned[:-1]], axis=0)
    around = jnp.where(iota((64, 8, 128), 1) < 4, above, below)
    half = jnp.where(lev == 0, turned, around).reshape(4, 2, 2, 4, 8, 128)
    blocks = jnp.where(iota((4, 2, 4, 8, 128), 4) < 64, half[:, :, 0], half[:, :, 1])
    for y in range(4):
        for x in range(4):
            s_buf[y * 4 + x] = blocks[y, :, x]

    local[1].wait()
    local[2].wait()
    u, v = cour_v[0], cour_v[1]
    east, north = wind_v[0] == 1, wind_v[1] == 1
    w_own[1, :, :, :COLS] = jnp.where(east, 0.0, u) + KAPPA
    w_own[2, :, :, :COLS] = jnp.where(east, u, 0.0) + KAPPA
    w_own[3, :, :, :COLS] = jnp.where(north, 0.0, v) + KAPPA
    w_own[4, :, :, :COLS] = jnp.where(north, v, 0.0) + KAPPA
    w_own[0, :, :, :COLS] = 1.0 - u - v - 4.0 * KAPPA
    lane = iota((ROWS, 128), 1)
    last, first = jnp.zeros((ROWS, 128), F32), jnp.zeros((ROWS, 128), F32)
    for e in range(4):
        for l in range(NLEV):
            k = e * NLEV + l
            last = jnp.where(lane == k, lroll(w_own[1 + e, l, :, COLS - 128 : COLS], k - 127), last)
            first = jnp.where(lane == k, lroll(w_own[1 + e, l, :, :128], k), first)
    col_s[0] = last
    col_s[1] = first
    for e in range(4):
        row_s[0, e] = w_own[1 + e, :, ROWS - 1, :COLS]
        row_s[1, e] = w_own[1 + e, :, 0, :COLS]

    pl.semaphore_wait(bar, len(greet))

    coef = [
        remote(row_s.at[0], row_r.at[0], coef_s.at[0], coef_r.at[0], near(0, 1)),
        remote(row_s.at[1], row_r.at[1], coef_s.at[1], coef_r.at[1], near(0, -1)),
        remote(col_s.at[0], col_r.at[0], coef_s.at[2], coef_r.at[2], near(1, 0)),
        remote(col_s.at[1], col_r.at[1], coef_s.at[3], coef_r.at[3], near(-1, 0)),
    ]
    for copy in coef:
        copy.start()
    stage1 = []
    for k in range(1, 16):
        other, device = in_plane(k)
        copy = remote(s_buf.at[other], i_buf.at[plane], st1_s.at[k], st1_r.at[k], device)
        copy.start()
        stage1.append(copy)
    i_buf[plane] = s_buf[plane]

    for copy in local[3:]:
        copy.wait()
    slot = iota((1, SLOTS), 1)
    cell = cells[0].astype(F32)
    row = jnp.floor(cell * (1.0 / COLS))
    col = cell - COLS * row
    sub = iota((ROWS, SLOTS), 0).astype(F32)
    row_mask = jnp.where(sub == row, 1.0, 0.0)
    onehot = jnp.where(iota((COLS, SLOTS), 0).astype(F32) == col, 1.0, 0.0).astype(BF16)
    weight = jnp.where(slot < counts[...], obs_w[0], 0.0)
    kern_rows = (kern[:, 0, 0, :][:, None, :] * row_mask[None]).reshape(NLEV * ROWS, SLOTS)
    kern_dense = exact_dot(kern_rows, onehot, ((1,), (1,))).reshape(NLEV, ROWS, COLS)
    level = iota((NLEV, ROWS, COLS), 0)
    prof_dense = jnp.zeros((NLEV, ROWS, COLS), F32)
    for l in range(NLEV):
        prof_dense = jnp.where(level == l, prof[l], prof_dense)
    kp = kern_dense * prof_dense

    for copy in stage1:
        copy.wait()
    lane6 = iota((2, 4, 8, 128), 3)
    for hi in range(2):
        low_y, high_y = i_buf_view(i_buf, hi)
        z_buf[2 * hi] = jnp.where(lane6 < 64, low_y, lroll(high_y, 64))
        z_buf[2 * hi + 1] = jnp.where(lane6 < 64, lroll(low_y, 64), high_y)
    stage2 = []
    for k in range(1, 4):
        to = lax.rem(tz + k, 4)
        copy = remote(z_buf.at[to], r_buf.at[tz], st2_s.at[k], st2_r.at[k], (face, ty * 16 + to * 4 + tx, lev))
        copy.start()
        stage2.append(copy)

    def halo_copy(side, to):
        there = lax.rem(face + (3 if side == 0 else 1), 4)
        src = (0, 0) if side == 0 else (1, 3)
        device = (there, ty * 16 + to * 4 + tx, lev)
        return remote(z_buf.at[(to, *src)], h_buf.at[side], hal_s.at[side, to], hal_r.at[side], device)

    @pl.when(tz == 0)
    def _():
        for to in range(4):
            halo_copy(0, to).start()

    @pl.when(tz == 3)
    def _():
        for to in range(4):
            halo_copy(1, to).start()

    r_buf[tz] = z_buf[tz]

    for copy in coef:
        copy.wait()
    right, left = col_r[1], col_r[0]
    for e in range(4):
        for l in range(NLEV):
            k = e * NLEV + l
            w_own[1 + e, l, :, COLS:] = jnp.where(
                lane == 0, lroll(right, -k), jnp.where(lane == 127, lroll(left, 127 - k), 0.0)
            )
    w_own[0, :, :, COLS:] = 1.0 - (
        w_own[1, :, :, COLS:] + w_own[2, :, :, COLS:] + w_own[3, :, :, COLS:] + w_own[4, :, :, COLS:]
    )
    sub2 = iota((ROWS, COLS), 0)
    is_up, is_down = (sub2 == 0) & (tile < 63), (sub2 == ROWS - 1) & (tile > 0)
    for l in range(NLEV):
        rest = jnp.where(is_up | is_down, 1.0, 0.0)
        for e in range(4):
            edge = jnp.where(is_up, row_r[1, e, l : l + 1], jnp.where(is_down, row_r[0, e, l : l + 1], 0.0))
            w_halo[1 + e, l] = edge
            rest = rest - edge
        w_halo[0, l] = rest

    stencil = {}

    def add(offset, term):
        stencil[offset] = stencil[offset] + term if offset in stencil else term

    for e1, (dy, dx) in enumerate(STEPS):
        g = kp * w_own[e1, :, :, :COLS]
        for e2, (ey, ex) in enumerate(STEPS):
            offset = (dy + ey, dx + ex)
            if dy == 0 and dx == 0:
                add(offset, jnp.sum(g * w_own[e2, :, :, :COLS], axis=0))
            elif dy == 0:
                h = lroll(jnp.concatenate([g, jnp.zeros((NLEV, ROWS, 128), F32)], axis=-1), dx)
                add(offset, lroll(jnp.sum(h * w_own[e2], axis=0), -dx)[:, :COLS])
            else:
                h, h_halo = rshift(g, jnp.zeros_like(g), dy)
                p, p_halo = jnp.sum(h * w_own[e2, :, :, :COLS], axis=0), jnp.sum(h_halo * w_halo[e2], axis=0)
                add(offset, rshift(p, p_halo, -dy)[0])
    spread = jnp.concatenate([stencil[o] for o in OFFSETS] + [jnp.zeros((3 * ROWS, COLS), F32)], axis=0)
    picked = exact_dot(spread, onehot, ((1,), (0,))).reshape(16, ROWS, SLOTS)
    l_buf[0] = jnp.sum(picked * row_mask[None], axis=1)
    to_peer = remote(l_buf.at[0], l_buf.at[1], lev_s, lev_r, peer)
    to_peer.start()
    to_peer.wait()

    sub16 = iota((16, SLOTS), 0)
    table = l_buf[0] + l_buf[1]
    table = jnp.where(sub16 == 13, observed[0], table)
    table = jnp.where(sub16 == 14, weight, table)
    slot_v[8:24] = jnp.where(sub16 == 15, cell, table)
    slot_v[0:8] = month[:, 0, 0, :]
    around_copies = []
    every = slot_v[...]
    lane24, sub24 = iota((PLANES, SLOTS), 1), iota((PLANES, SLOTS), 0)
    for k, corner in enumerate((0.0, COLS - 1.0, (ROWS - 1.0) * COLS, ROWS * COLS - 1.0)):
        found = jnp.sum(jnp.where(cell == corner, every, 0.0), axis=1, keepdims=True)
        line = jnp.sum(jnp.where(lane24 == sub24 + 32 * k, found, 0.0), axis=0, keepdims=True)
        corner_s[k] = jnp.broadcast_to(line, (8, SLOTS))
    for k, d in enumerate(sends):
        src, dst = (slot_v, nb.at[k]) if k < 4 else (corner_s.at[k - 4, pl.ds(0, 1)], corner_r.at[k - 4, pl.ds(0, 1)])
        copy = remote(src, dst, nb_s.at[k], nb_r.at[k], near(*d))
        copy.start()
        around_copies.append(copy)

    def rows_of(values, mask):
        return (values[:, None, :] * mask[None]).reshape(PLANES * ROWS, SLOTS)

    own = exact_dot(rows_of(slot_v[...], row_mask), onehot, ((1,), (1,)))
    dense[0, :, :, :COLS] = own.reshape(PLANES, ROWS, COLS)

    for copy in around_copies:
        copy.wait()
    up, down = tile < 63, tile > 0

    def place(k):
        c = nb[k, 23:24, :]
        r = jnp.floor(c * (1.0 / COLS))
        return r, c - COLS * r

    def near_rows(r, upper):
        keep = (r <= 1.0) & up if upper else (r >= 6.0) & down
        return jnp.where((sub == r) & keep, 1.0, 0.0)

    def near_cols(c, righter):
        target = iota((128, SLOTS), 0).astype(F32)
        hit = (target == c) & (c <= 1.0) if righter else (target == c - (COLS - 128.0)) & (c >= COLS - 2.0)
        return jnp.where(hit, 1.0, 0.0).astype(BF16)

    values, hots = [], []
    for k, upper in ((0, True), (1, False)):
        r, c = place(k)
        values.append(rows_of(nb[k], near_rows(r, upper)))
        hots.append(jnp.where(iota((COLS, SLOTS), 0).astype(F32) == c, 1.0, 0.0).astype(BF16))
    out = exact_dot(jnp.concatenate(values, axis=1), jnp.concatenate(hots, axis=1), ((1,), (1,)))
    dense[1, :, :, :COLS] = out.reshape(PLANES, ROWS, COLS)
    values, hots = [], []
    for k, righter in ((2, True), (3, False)):
        r, c = place(k)
        values.append(rows_of(nb[k], jnp.where(sub == r, 1.0, 0.0)))
        hots.append(near_cols(c, righter))
    out = exact_dot(jnp.concatenate(values, axis=1), jnp.concatenate(hots, axis=1), ((1,), (1,)))
    dense[0, :, :, COLS:] = out.reshape(PLANES, ROWS, 128)
    corners = corner_r[0, 0:1] + corner_r[1, 0:1] + corner_r[2, 0:1] + corner_r[3, 0:1]
    corners = jnp.where(lane24 % 32 == sub24, corners, 0.0)
    mask = jnp.where(((lane < 64) & (sub == 0.0) & up) | ((lane >= 64) & (sub == ROWS - 1.0) & down), 1.0, 0.0)
    place0, side = iota((128, SLOTS), 0), (iota((128, SLOTS), 1) // 32) % 2
    hot = jnp.where(place0 == 127 * side, 1.0, 0.0).astype(BF16)
    out = exact_dot(rows_of(corners, mask), hot, ((1,), (1,)))
    dense[1, :, :, COLS:] = out.reshape(PLANES, ROWS, 128)

    for dx in range(-2, 3):
        months = lroll(dense[0, 0:8], dx), lroll(dense[1, 0:8], dx)
        for i, (oy, ox) in enumerate(OFFSETS):
            if ox == dx:
                m_own, m_halo = rshift(*months, oy)
                m_sh[i, 0] = m_own
                m_sh[i, 1] = m_halo
                a_own, a_halo = rshift(lroll(dense[0, 8 + i], dx), lroll(dense[1, 8 + i], dx), oy)
                a_sh[i, 0] = a_own
                a_sh[i, 1] = a_halo

    for copy in stage2:
        copy.wait()

    @pl.when(tz == 0)
    def _():
        for to in range(4):
            halo_copy(0, to).wait_send()

    @pl.when(tz == 3)
    def _():
        for to in range(4):
            halo_copy(1, to).wait_send()

    for side in range(2):
        halo_copy(side, 0).wait_recv()
    parts = [r_buf[i // 4, :, i % 4] for i in range(16)]
    lanes = iota((2, 8, 128), 2)
    for step in (1, 2, 4, 8):
        upper_half = (lanes // (8 * step)) % 2 == 1
        for i in range(16):
            if i & step == 0:
                a, b = parts[i], parts[i + step]
                parts[i] = jnp.where(upper_half, lroll(b, 8 * step), a)
                parts[i + step] = jnp.where(upper_half, b, lroll(a, -8 * step))
    for g in range(16):
        for y in range(2):
            f_buf[lev, g % 8, :, (2 * y + g // 8) * 128 : (2 * y + g // 8 + 1) * 128] = parts[g][y]
    for t in range(NT):
        f_buf[lev, t, :, COLS:] = jnp.where(
            lane < 4, lroll(h_buf[0], -8 * t), jnp.where(lane >= 124, lroll(h_buf[1], 56 - 8 * t), 0.0)
        )
    swap = remote(f_buf.at[lev], f_buf.at[lev], fx_s, fx_r, peer)
    swap.start()
    swap.wait()

    by_row = {}
    for i, (dy, dx) in enumerate(OFFSETS):
        pair = tuple(lroll(a_sh[i, h] * jnp.sum(m_sh[i, h] * f_buf[h], axis=0), -dx) for h in range(2))
        by_row[dy] = tuple(p + q for p, q in zip(by_row[dy], pair)) if dy in by_row else pair
    model = None
    for dy, pair in by_row.items():
        pair = rshift(*pair, -dy)
        model = pair if model is None else tuple(p + q for p, q in zip(model, pair))
    forcing = tuple(dense[h, 22] * (dense[h, 21] - model[h]) for h in range(2))
    adj = jnp.zeros((NT, ROWS, COLS), F32)
    for dx in range(-2, 3):
        moved = tuple(lroll(f, dx) for f in forcing)
        for i, (oy, ox) in enumerate(OFFSETS):
            if ox == dx:
                q = (a_sh[i, 0] * rshift(*moved, oy)[0])[:, :COLS]
                adj = adj + q[None] * m_sh[i, 0, :, :, :COLS]

    square = adj * adj
    square = square[..., :128] + square[..., 128:256] + square[..., 256:384] + square[..., 384:]
    square = jnp.sum(square, axis=1)
    for by in (64, 32, 16):
        square = square + lroll(square, by)
    mine = jnp.where(lane // 16 == iota((ROWS, 128), 0), square, 0.0)
    az[z] = jnp.broadcast_to(jnp.sum(mine, axis=0, keepdims=True), (8, 128))
    copies = []
    for k in range(1, 16):
        copy = remote(az.at[z, pl.ds(0, 1)], az.at[z, pl.ds(0, 1)], az_s.at[k], az_r.at[k], in_line(k))
        copy.start()
        copies.append(copy)
    for t in range(NT):
        fg_out[t] = prec[t] * f_buf[0, t, :, :COLS] - adj[t]
    for copy in copies:
        copy.wait()
    total = az[0, 0:1]
    for i in range(1, 16):
        total = total + az[i, 0:1]
    ap[plane] = jnp.broadcast_to(total, (8, 128))
    copies = []
    for k in range(1, 16):
        copy = remote(ap.at[plane, pl.ds(0, 1)], ap.at[plane, pl.ds(0, 1)], ap_s.at[k], ap_r.at[k], in_plane(k)[1])
        copy.start()
        copies.append(copy)
    for copy in copies:
        copy.wait()
    total = ap[0, 0:1]
    for i in range(1, 16):
        total = total + ap[i, 0:1]
    sums = jnp.sum(jnp.where(lane // 16 == iota((ROWS, 128), 0), total, 0.0), axis=1, keepdims=True)
    sums = jnp.sum(jnp.where(lane == iota((ROWS, 128), 0), sums, 0.0), axis=0, keepdims=True)[:, :NT]
    p = prec_v[...].reshape(1, NT)
    pg_out[...] = (0.5 / p - 0.5 * (sums / all_cells) / (p * p)).reshape(NT)


def i_buf_view(i_buf, hi):
    low = jnp.concatenate([i_buf[0:4, hi][None], i_buf[8:12, hi][None]], axis=0)
    high = jnp.concatenate([i_buf[4:8, hi][None], i_buf[12:16, hi][None]], axis=0)
    return low, high


def on_device(flux, profile, courant, winds, cells, counts, kernels, month_weight, observed, obs_weight, precision):
    vmem = pl.BlockSpec(memory_space=pltpu.VMEM)
    hbm = pl.BlockSpec(memory_space=pltpu.HBM)
    dma = pltpu.SemaphoreType.DMA

    def buf(*shape, dtype=F32):
        return pltpu.VMEM(shape, dtype)

    def smem(*shape, dtype=F32):
        return pltpu.SMEM(shape, dtype)

    all_cells = float(ROWS * COLS * lax.axis_size("tile") * lax.axis_size("face"))
    return pl.pallas_call(
        functools.partial(main_kernel, all_cells),
        name="gradient",
        out_shape=(jax.ShapeDtypeStruct((NT, ROWS, COLS), F32), jax.ShapeDtypeStruct((NT,), F32)),
        in_specs=[hbm] * 10 + [vmem],
        out_specs=(vmem, vmem),
        scratch_shapes=[
            smem(NLEV), buf(1, 1, SLOTS, dtype=jnp.int32), buf(NLEV, 1, 1, SLOTS), buf(NT, 1, 1, SLOTS),
            buf(1, 1, SLOTS), buf(1, 1, SLOTS), smem(NT), buf(NT),
            buf(8, NT, 512), buf(2, NLEV, ROWS, COLS), buf(2, NLEV, ROWS, COLS, dtype=jnp.int32),
            buf(5, NLEV, ROWS, WIDE), buf(5, NLEV, ROWS, COLS), buf(2, 4, NLEV, COLS), buf(2, 4, NLEV, COLS),
            buf(2, 8, 128), buf(2, 8, 128),
            buf(16, 2, 8, 128), buf(16, 2, 8, 128), buf(4, 2, 4, 8, 128), buf(4, 2, 4, 8, 128), buf(2, 8, 128),
            buf(2, NT, ROWS, WIDE),
            buf(2, 16, SLOTS), buf(PLANES, SLOTS), buf(4, PLANES, SLOTS), buf(4, 8, SLOTS), buf(4, 8, SLOTS),
            buf(2, PLANES, ROWS, WIDE),
            buf(N_OFF, 2, NT, ROWS, WIDE), buf(N_OFF, 2, ROWS, WIDE), buf(16, 8, 128), buf(16, 8, 128),
            dma((11,)), dma((4,)), dma((4,)), dma((16,)), dma((16,)), dma((4,)), dma((4,)), dma((2, 4)), dma((2,)), dma, dma,
            dma, dma, dma((8,)), dma((8,)), dma((16,)), dma((16,)), dma((16,)), dma((16,)),
        ],
        compiler_params=pltpu.CompilerParams(collective_id=0, has_side_effects=True, vmem_limit_bytes=40 * 2**20),
    )(
        *(
            pltpu.with_memory_space_constraint(x, pltpu.HBM)
            for x in (flux, profile, courant, winds, cells, kernels, month_weight, observed, obs_weight, precision)
        ),
        jnp.broadcast_to(counts, (1, SLOTS)),
    )


def solution(mesh):
    return jax.shard_map(
        on_device,
        mesh=mesh,
        in_specs=(
            P(("face", "tile"), None, None),
            P("lev"),
            P(None, "lev", "tile", "face"),
            P(None, "lev", "tile", "face"),
            P("tile", "face", None),
            P("tile", "face"),
            P("lev", "tile", "face", None),
            P(None, "tile", "face", None),
            P("tile", "face", None),
            P("tile", "face", None),
            P(),
        ),
        out_specs=(P(None, "tile", "face"), P()),
        check_vma=False,
    )
```

```python
import functools

import jax
import jax.numpy as jnp
from jax import lax
from jax.experimental import pallas as pl
from jax.experimental.pallas import tpu as pltpu
from jax.sharding import PartitionSpec as P

KAPPA = 0.025
MESH = pl.DeviceIdType.MESH
F32 = jnp.float32
BF16 = jnp.bfloat16

NT, NLEV, ROWS, COLS, SLOTS = 8, 8, 8, 512, 128
WIDE = COLS + 128
STEPS = ((0, 0), (0, -1), (0, 1), (-1, 0), (1, 0))
OFFSETS = tuple((dy, dx) for dy in range(-2, 3) for dx in range(-2, 3) if abs(dy) + abs(dx) <= 2)
N_OFF = len(OFFSETS)
PLANES = 24


def iota(shape, dim):
    return lax.broadcasted_iota(jnp.int32, shape, dim)


def lroll(x, by):
    by = by % x.shape[-1]
    return x if by == 0 else pltpu.roll(x, by, x.ndim - 1)


def rshift(own, halo, by):
    if by == 0:
        return own, halo
    axis = own.ndim - 2
    turned_own = pltpu.roll(own, by % ROWS, axis)
    turned_halo = pltpu.roll(halo, by % ROWS, axis)
    sub = iota(own.shape, axis)
    cross = sub < by if by > 0 else sub >= ROWS + by
    return jnp.where(cross, turned_halo, turned_own), jnp.where(cross, turned_own, turned_halo)


def exact_dot(values, onehot, dims):
    high = values.astype(BF16)
    rest = values - high.astype(F32)
    middle = rest.astype(BF16)
    low = (rest - middle.astype(F32)).astype(BF16)
    dot = lambda part: lax.dot_general(part, onehot, (dims, ((), ())), preferred_element_type=F32)
    return dot(high) + (dot(middle) + dot(low))


def remote(src, dst, send, recv, device):
    return pltpu.make_async_remote_copy(
        src_ref=src, dst_ref=dst, send_sem=send, recv_sem=recv, device_id=device, device_id_type=MESH
    )


def main_kernel(
    all_cells,
    flux_h, prof_h, cour_h, wind_h, cells_h, kern_h, month_h, observed_h, obs_w_h, prec_h, counts,
    fg_out, pg_out,
    prof, cells, kern, month, observed, obs_w, prec, prec_v,
    flux_v, cour_v, wind_v, w_own, w_halo, row_s, row_r, col_s, col_r,
    s_buf, i_buf, z_buf, r_buf, h_buf, f_buf,
    l_buf, slot_v, nb, corner_s, corner_r, dense, m_sh, a_sh, az, ap,
    loc_sem, coef_s, coef_r, st1_s, st1_r, st2_s, st2_r, hal_s, hal_r, fx_s, fx_r,
    lev_s, lev_r, nb_s, nb_r, az_s, az_r, ap_s, ap_r,
):
    face, tile, lev = lax.axis_index("face"), lax.axis_index("tile"), lax.axis_index("lev")
    ty, tz, tx = tile // 16, (tile // 4) % 4, tile % 4
    z, plane = tz * 4 + face, ty * 4 + tx

    def in_plane(k):
        other = lax.rem(plane + k, 16)
        return other, (face, (other // 4) * 16 + tz * 4 + other % 4, lev)

    def in_line(k):
        other = lax.rem(z + k, 16)
        return (other % 4, ty * 16 + (other // 4) * 4 + tx, lev)

    def near(df, dt):
        return (lax.rem(face + 4 + df, 4), lax.rem(tile + 64 + dt, 64), lev)

    peer = (face, tile, 1 - lev)
    sends = ((0, -1), (0, 1), (-1, 0), (1, 0), (-1, -1), (1, -1), (-1, 1), (1, 1))

    bar = pltpu.get_barrier_semaphore()
    greet = [peer] + [in_line(k) for k in range(1, 16)] + [in_plane(k)[1] for k in range(1, 16)]
    greet += [near(*d) for d in sends if d[1] != 0]
    for device in greet:
        pl.semaphore_signal(bar, inc=1, device_id=device, device_id_type=MESH)

    local = [
        pltpu.make_async_copy(src, dst, loc_sem.at[i])
        for i, (src, dst) in enumerate(
            (
                (flux_h, flux_v), (cour_h, cour_v), (wind_h, wind_v), (cells_h, cells), (kern_h, kern),
                (prof_h, prof), (obs_w_h, obs_w), (observed_h, observed), (month_h, month), (prec_h, prec), (prec_h, prec_v),
            )
        )
    ]
    for copy in local:
        copy.start()

    local[0].wait()
    by_tracer = jnp.swapaxes(flux_v[...], 0, 1).reshape(NT * 8, 512)
    turned = jnp.transpose(jnp.concatenate([by_tracer, by_tracer], axis=0)).reshape(64, 8, 128)
    nothing = jnp.zeros((1, 8, 128), F32)
    above = jnp.concatenate([turned[1:], nothing], axis=0)
    below = jnp.concatenate([nothing, turned[:-1]], axis=0)
    around = jnp.where(iota((64, 8, 128), 1) < 4, above, below)
    half = jnp.where(lev == 0, turned, around).reshape(4, 2, 2, 4, 8, 128)
    blocks = jnp.where(iota((4, 2, 4, 8, 128), 4) < 64, half[:, :, 0], half[:, :, 1])
    for y in range(4):
        for x in range(4):
            s_buf[y * 4 + x] = blocks[y, :, x]

    local[1].wait()
    local[2].wait()
    u, v = cour_v[0], cour_v[1]
    east, north = wind_v[0] == 1, wind_v[1] == 1
    w_own[1, :, :, :COLS] = jnp.where(east, 0.0, u) + KAPPA
    w_own[2, :, :, :COLS] = jnp.where(east, u, 0.0) + KAPPA
    w_own[3, :, :, :COLS] = jnp.where(north, 0.0, v) + KAPPA
    w_own[4, :, :, :COLS] = jnp.where(north, v, 0.0) + KAPPA
    w_own[0, :, :, :COLS] = 1.0 - u - v - 4.0 * KAPPA
    lane = iota((ROWS, 128), 1)
    last, first = jnp.zeros((ROWS, 128), F32), jnp.zeros((ROWS, 128), F32)
    for e in range(4):
        for l in range(NLEV):
            k = e * NLEV + l
            last = jnp.where(lane == k, lroll(w_own[1 + e, l, :, COLS - 128 : COLS], k - 127), last)
            first = jnp.where(lane == k, lroll(w_own[1 + e, l, :, :128], k), first)
    col_s[0] = last
    col_s[1] = first
    for e in range(4):
        row_s[0, e] = w_own[1 + e, :, ROWS - 1, :COLS]
        row_s[1, e] = w_own[1 + e, :, 0, :COLS]

    pl.semaphore_wait(bar, len(greet))

    coef = [
        remote(row_s.at[0], row_r.at[0], coef_s.at[0], coef_r.at[0], near(0, 1)),
        remote(row_s.at[1], row_r.at[1], coef_s.at[1], coef_r.at[1], near(0, -1)),
        remote(col_s.at[0], col_r.at[0], coef_s.at[2], coef_r.at[2], near(1, 0)),
        remote(col_s.at[1], col_r.at[1], coef_s.at[3], coef_r.at[3], near(-1, 0)),
    ]
    for copy in coef:
        copy.start()
    stage1 = []
    for k in range(1, 16):
        other, device = in_plane(k)
        copy = remote(s_buf.at[other], i_buf.at[plane], st1_s.at[k], st1_r.at[k], device)
        copy.start()
        stage1.append(copy)
    i_buf[plane] = s_buf[plane]

    for copy in local[3:]:
        copy.wait()
    slot = iota((1, SLOTS), 1)
    cell = cells[0].astype(F32)
    row = jnp.floor(cell * (1.0 / COLS))
    col = cell - COLS * row
    sub = iota((ROWS, SLOTS), 0).astype(F32)
    row_mask = jnp.where(sub == row, 1.0, 0.0)
    onehot = jnp.where(iota((COLS, SLOTS), 0).astype(F32) == col, 1.0, 0.0).astype(BF16)
    weight = jnp.where(slot < counts[...], obs_w[0], 0.0)
    kern_rows = (kern[:, 0, 0, :][:, None, :] * row_mask[None]).reshape(NLEV * ROWS, SLOTS)
    kern_dense = exact_dot(kern_rows, onehot, ((1,), (1,))).reshape(NLEV, ROWS, COLS)
    level = iota((NLEV, ROWS, COLS), 0)
    prof_dense = jnp.zeros((NLEV, ROWS, COLS), F32)
    for l in range(NLEV):
        prof_dense = jnp.where(level == l, prof[l], prof_dense)
    kp = kern_dense * prof_dense

    for copy in stage1:
        copy.wait()
    lane6 = iota((2, 4, 8, 128), 3)
    for hi in range(2):
        low_y, high_y = i_buf_view(i_buf, hi)
        z_buf[2 * hi] = jnp.where(lane6 < 64, low_y, lroll(high_y, 64))
        z_buf[2 * hi + 1] = jnp.where(lane6 < 64, lroll(low_y, 64), high_y)
    stage2 = []
    for k in range(1, 4):
        to = lax.rem(tz + k, 4)
        copy = remote(z_buf.at[to], r_buf.at[tz], st2_s.at[k], st2_r.at[k], (face, ty * 16 + to * 4 + tx, lev))
        copy.start()
        stage2.append(copy)

    def halo_copy(side, to):
        there = lax.rem(face + (3 if side == 0 else 1), 4)
        src = (0, 0) if side == 0 else (1, 3)
        device = (there, ty * 16 + to * 4 + tx, lev)
        return remote(z_buf.at[(to, *src)], h_buf.at[side], hal_s.at[side, to], hal_r.at[side], device)

    @pl.when(tz == 0)
    def _():
        for to in range(4):
            halo_copy(0, to).start()

    @pl.when(tz == 3)
    def _():
        for to in range(4):
            halo_copy(1, to).start()

    r_buf[tz] = z_buf[tz]

    for copy in coef:
        copy.wait()
    right, left = col_r[1], col_r[0]
    for e in range(4):
        for l in range(NLEV):
            k = e * NLEV + l
            w_own[1 + e, l, :, COLS:] = jnp.where(
                lane == 0, lroll(right, -k), jnp.where(lane == 127, lroll(left, 127 - k), 0.0)
            )
    w_own[0, :, :, COLS:] = 1.0 - (
        w_own[1, :, :, COLS:] + w_own[2, :, :, COLS:] + w_own[3, :, :, COLS:] + w_own[4, :, :, COLS:]
    )
    sub2 = iota((ROWS, COLS), 0)
    is_up, is_down = (sub2 == 0) & (tile < 63), (sub2 == ROWS - 1) & (tile > 0)
    for l in range(NLEV):
        rest = jnp.where(is_up | is_down, 1.0, 0.0)
        for e in range(4):
            edge = jnp.where(is_up, row_r[1, e, l : l + 1], jnp.where(is_down, row_r[0, e, l : l + 1], 0.0))
            w_halo[1 + e, l] = edge
            rest = rest - edge
        w_halo[0, l] = rest

    stencil = {}

    def add(offset, term):
        stencil[offset] = stencil[offset] + term if offset in stencil else term

    for e1, (dy, dx) in enumerate(STEPS):
        g = kp * w_own[e1, :, :, :COLS]
        for e2, (ey, ex) in enumerate(STEPS):
            offset = (dy + ey, dx + ex)
            if dy == 0 and dx == 0:
                add(offset, jnp.sum(g * w_own[e2, :, :, :COLS], axis=0))
            elif dy == 0:
                h = lroll(jnp.concatenate([g, jnp.zeros((NLEV, ROWS, 128), F32)], axis=-1), dx)
                add(offset, lroll(jnp.sum(h * w_own[e2], axis=0), -dx)[:, :COLS])
            else:
                h, h_halo = rshift(g, jnp.zeros_like(g), dy)
                p, p_halo = jnp.sum(h * w_own[e2, :, :, :COLS], axis=0), jnp.sum(h_halo * w_halo[e2], axis=0)
                add(offset, rshift(p, p_halo, -dy)[0])
    spread = jnp.concatenate([stencil[o] for o in OFFSETS] + [jnp.zeros((3 * ROWS, COLS), F32)], axis=0)
    picked = exact_dot(spread, onehot, ((1,), (0,))).reshape(16, ROWS, SLOTS)
    l_buf[0] = jnp.sum(picked * row_mask[None], axis=1)
    to_peer = remote(l_buf.at[0], l_buf.at[1], lev_s, lev_r, peer)
    to_peer.start()
    to_peer.wait()

    sub16 = iota((16, SLOTS), 0)
    table = l_buf[0] + l_buf[1]
    table = jnp.where(sub16 == 13, observed[0], table)
    table = jnp.where(sub16 == 14, weight, table)
    slot_v[8:24] = jnp.where(sub16 == 15, cell, table)
    slot_v[0:8] = month[:, 0, 0, :]
    around_copies = []
    every = slot_v[...]
    lane24, sub24 = iota((PLANES, SLOTS), 1), iota((PLANES, SLOTS), 0)
    for k, corner in enumerate((0.0, COLS - 1.0, (ROWS - 1.0) * COLS, ROWS * COLS - 1.0)):
        found = jnp.sum(jnp.where(cell == corner, every, 0.0), axis=1, keepdims=True)
        line = jnp.sum(jnp.where(lane24 == sub24 + 32 * k, found, 0.0), axis=0, keepdims=True)
        corner_s[k] = jnp.broadcast_to(line, (8, SLOTS))
    for k, d in enumerate(sends):
        src, dst = (slot_v, nb.at[k]) if k < 4 else (corner_s.at[k - 4, pl.ds(0, 1)], corner_r.at[k - 4, pl.ds(0, 1)])
        copy = remote(src, dst, nb_s.at[k], nb_r.at[k], near(*d))
        copy.start()
        around_copies.append(copy)

    def rows_of(values, mask):
        return (values[:, None, :] * mask[None]).reshape(PLANES * ROWS, SLOTS)

    own = exact_dot(rows_of(slot_v[...], row_mask), onehot, ((1,), (1,)))
    dense[0, :, :, :COLS] = own.reshape(PLANES, ROWS, COLS)

    for copy in stage2:
        copy.wait()

    @pl.when(tz == 0)
    def _():
        for to in range(4):
            halo_copy(0, to).wait_send()

    @pl.when(tz == 3)
    def _():
        for to in range(4):
            halo_copy(1, to).wait_send()

    for side in range(2):
        halo_copy(side, 0).wait_recv()
    parts = [r_buf[i // 4, :, i % 4] for i in range(16)]
    lanes = iota((2, 8, 128), 2)
    for step in (1, 2, 4, 8):
        upper_half = (lanes // (8 * step)) % 2 == 1
        for i in range(16):
            if i & step == 0:
                a, b = parts[i], parts[i + step]
                parts[i] = jnp.where(upper_half, lroll(b, 8 * step), a)
                parts[i + step] = jnp.where(upper_half, b, lroll(a, -8 * step))
    for g in range(16):
        for y in range(2):
            f_buf[lev, g % 8, :, (2 * y + g // 8) * 128 : (2 * y + g // 8 + 1) * 128] = parts[g][y]
    for t in range(NT):
        f_buf[lev, t, :, COLS:] = jnp.where(
            lane < 4, lroll(h_buf[0], -8 * t), jnp.where(lane >= 124, lroll(h_buf[1], 56 - 8 * t), 0.0)
        )
    swap = remote(f_buf.at[lev], f_buf.at[lev], fx_s, fx_r, peer)
    swap.start()

    for copy in around_copies:
        copy.wait()
    up, down = tile < 63, tile > 0

    def place(k):
        c = nb[k, 23:24, :]
        r = jnp.floor(c * (1.0 / COLS))
        return r, c - COLS * r

    def near_rows(r, upper):
        keep = (r <= 1.0) & up if upper else (r >= 6.0) & down
        return jnp.where((sub == r) & keep, 1.0, 0.0)

    def near_cols(c, righter):
        target = iota((128, SLOTS), 0).astype(F32)
        hit = (target == c) & (c <= 1.0) if righter else (target == c - (COLS - 128.0)) & (c >= COLS - 2.0)
        return jnp.where(hit, 1.0, 0.0).astype(BF16)

    values, hots = [], []
    for k, upper in ((0, True), (1, False)):
        r, c = place(k)
        values.append(rows_of(nb[k], near_rows(r, upper)))
        hots.append(jnp.where(iota((COLS, SLOTS), 0).astype(F32) == c, 1.0, 0.0).astype(BF16))
    out = exact_dot(jnp.concatenate(values, axis=1), jnp.concatenate(hots, axis=1), ((1,), (1,)))
    dense[1, :, :, :COLS] = out.reshape(PLANES, ROWS, COLS)
    values, hots = [], []
    for k, righter in ((2, True), (3, False)):
        r, c = place(k)
        values.append(rows_of(nb[k], jnp.where(sub == r, 1.0, 0.0)))
        hots.append(near_cols(c, righter))
    out = exact_dot(jnp.concatenate(values, axis=1), jnp.concatenate(hots, axis=1), ((1,), (1,)))
    dense[0, :, :, COLS:] = out.reshape(PLANES, ROWS, 128)
    corners = corner_r[0, 0:1] + corner_r[1, 0:1] + corner_r[2, 0:1] + corner_r[3, 0:1]
    corners = jnp.where(lane24 % 32 == sub24, corners, 0.0)
    mask = jnp.where(((lane < 64) & (sub == 0.0) & up) | ((lane >= 64) & (sub == ROWS - 1.0) & down), 1.0, 0.0)
    place0, side = iota((128, SLOTS), 0), (iota((128, SLOTS), 1) // 32) % 2
    hot = jnp.where(place0 == 127 * side, 1.0, 0.0).astype(BF16)
    out = exact_dot(rows_of(corners, mask), hot, ((1,), (1,)))
    dense[1, :, :, COLS:] = out.reshape(PLANES, ROWS, 128)

    for dx in range(-2, 3):
        months = lroll(dense[0, 0:8], dx), lroll(dense[1, 0:8], dx)
        for i, (oy, ox) in enumerate(OFFSETS):
            if ox == dx:
                m_own, m_halo = rshift(*months, oy)
                m_sh[i, 0] = m_own
                m_sh[i, 1] = m_halo
                a_own, a_halo = rshift(lroll(dense[0, 8 + i], dx), lroll(dense[1, 8 + i], dx), oy)
                a_sh[i, 0] = a_own
                a_sh[i, 1] = a_halo

    swap.wait()

    by_row = {}
    for i, (dy, dx) in enumerate(OFFSETS):
        pair = tuple(lroll(a_sh[i, h] * jnp.sum(m_sh[i, h] * f_buf[h], axis=0), -dx) for h in range(2))
        by_row[dy] = tuple(p + q for p, q in zip(by_row[dy], pair)) if dy in by_row else pair
    model = None
    for dy, pair in by_row.items():
        pair = rshift(*pair, -dy)
        model = pair if model is None else tuple(p + q for p, q in zip(model, pair))
    forcing = tuple(dense[h, 22] * (dense[h, 21] - model[h]) for h in range(2))
    adj = jnp.zeros((NT, ROWS, COLS), F32)
    for dx in range(-2, 3):
        moved = tuple(lroll(f, dx) for f in forcing)
        for i, (oy, ox) in enumerate(OFFSETS):
            if ox == dx:
                q = (a_sh[i, 0] * rshift(*moved, oy)[0])[:, :COLS]
                adj = adj + q[None] * m_sh[i, 0, :, :, :COLS]

    square = adj * adj
    square = square[..., :128] + square[..., 128:256] + square[..., 256:384] + square[..., 384:]
    square = jnp.sum(square, axis=1)
    for by in (64, 32, 16):
        square = square + lroll(square, by)
    mine = jnp.where(lane // 16 == iota((ROWS, 128), 0), square, 0.0)
    az[z] = jnp.broadcast_to(jnp.sum(mine, axis=0, keepdims=True), (8, 128))
    copies = []
    for k in range(1, 16):
        copy = remote(az.at[z, pl.ds(0, 1)], az.at[z, pl.ds(0, 1)], az_s.at[k], az_r.at[k], in_line(k))
        copy.start()
        copies.append(copy)
    for t in range(NT):
        fg_out[t] = prec[t] * f_buf[0, t, :, :COLS] - adj[t]
    for copy in copies:
        copy.wait()
    total = az[0, 0:1]
    for i in range(1, 16):
        total = total + az[i, 0:1]
    ap[plane] = jnp.broadcast_to(total, (8, 128))
    copies = []
    for k in range(1, 16):
        copy = remote(ap.at[plane, pl.ds(0, 1)], ap.at[plane, pl.ds(0, 1)], ap_s.at[k], ap_r.at[k], in_plane(k)[1])
        copy.start()
        copies.append(copy)
    for copy in copies:
        copy.wait()
    total = ap[0, 0:1]
    for i in range(1, 16):
        total = total + ap[i, 0:1]
    sums = jnp.sum(jnp.where(lane // 16 == iota((ROWS, 128), 0), total, 0.0), axis=1, keepdims=True)
    sums = jnp.sum(jnp.where(lane == iota((ROWS, 128), 0), sums, 0.0), axis=0, keepdims=True)[:, :NT]
    p = prec_v[...].reshape(1, NT)
    pg_out[...] = (0.5 / p - 0.5 * (sums / all_cells) / (p * p)).reshape(NT)


def i_buf_view(i_buf, hi):
    low = jnp.concatenate([i_buf[0:4, hi][None], i_buf[8:12, hi][None]], axis=0)
    high = jnp.concatenate([i_buf[4:8, hi][None], i_buf[12:16, hi][None]], axis=0)
    return low, high


def on_device(flux, profile, courant, winds, cells, counts, kernels, month_weight, observed, obs_weight, precision):
    vmem = pl.BlockSpec(memory_space=pltpu.VMEM)
    hbm = pl.BlockSpec(memory_space=pltpu.HBM)
    dma = pltpu.SemaphoreType.DMA

    def buf(*shape, dtype=F32):
        return pltpu.VMEM(shape, dtype)

    def smem(*shape, dtype=F32):
        return pltpu.SMEM(shape, dtype)

    all_cells = float(ROWS * COLS * lax.axis_size("tile") * lax.axis_size("face"))
    return pl.pallas_call(
        functools.partial(main_kernel, all_cells),
        name="gradient",
        out_shape=(jax.ShapeDtypeStruct((NT, ROWS, COLS), F32), jax.ShapeDtypeStruct((NT,), F32)),
        in_specs=[hbm] * 10 + [vmem],
        out_specs=(vmem, vmem),
        scratch_shapes=[
            smem(NLEV), buf(1, 1, SLOTS, dtype=jnp.int32), buf(NLEV, 1, 1, SLOTS), buf(NT, 1, 1, SLOTS),
            buf(1, 1, SLOTS), buf(1, 1, SLOTS), smem(NT), buf(NT),
            buf(8, NT, 512), buf(2, NLEV, ROWS, COLS), buf(2, NLEV, ROWS, COLS, dtype=jnp.int32),
            buf(5, NLEV, ROWS, WIDE), buf(5, NLEV, ROWS, COLS), buf(2, 4, NLEV, COLS), buf(2, 4, NLEV, COLS),
            buf(2, 8, 128), buf(2, 8, 128),
            buf(16, 2, 8, 128), buf(16, 2, 8, 128), buf(4, 2, 4, 8, 128), buf(4, 2, 4, 8, 128), buf(2, 8, 128),
            buf(2, NT, ROWS, WIDE),
            buf(2, 16, SLOTS), buf(PLANES, SLOTS), buf(4, PLANES, SLOTS), buf(4, 8, SLOTS), buf(4, 8, SLOTS),
            buf(2, PLANES, ROWS, WIDE),
            buf(N_OFF, 2, NT, ROWS, WIDE), buf(N_OFF, 2, ROWS, WIDE), buf(16, 8, 128), buf(16, 8, 128),
            dma((11,)), dma((4,)), dma((4,)), dma((16,)), dma((16,)), dma((4,)), dma((4,)), dma((2, 4)), dma((2,)), dma, dma,
            dma, dma, dma((8,)), dma((8,)), dma((16,)), dma((16,)), dma((16,)), dma((16,)),
        ],
        compiler_params=pltpu.CompilerParams(collective_id=0, has_side_effects=True, vmem_limit_bytes=40 * 2**20),
    )(
        *(
            pltpu.with_memory_space_constraint(x, pltpu.HBM)
            for x in (flux, profile, courant, winds, cells, kernels, month_weight, observed, obs_weight, precision)
        ),
        jnp.broadcast_to(counts, (1, SLOTS)),
    )


def solution(mesh):
    return jax.shard_map(
        on_device,
        mesh=mesh,
        in_specs=(
            P(("face", "tile"), None, None),
            P("lev"),
            P(None, "lev", "tile", "face"),
            P(None, "lev", "tile", "face"),
            P("tile", "face", None),
            P("tile", "face"),
            P("lev", "tile", "face", None),
            P(None, "tile", "face", None),
            P("tile", "face", None),
            P("tile", "face", None),
            P(),
        ),
        out_specs=(P(None, "tile", "face"), P()),
        check_vma=False,
    )
```

```python
import functools

import jax
import jax.numpy as jnp
from jax import lax
from jax.experimental import pallas as pl
from jax.experimental.pallas import tpu as pltpu
from jax.sharding import PartitionSpec as P

KAPPA = 0.025
MESH = pl.DeviceIdType.MESH
F32 = jnp.float32
BF16 = jnp.bfloat16

NT, NLEV, ROWS, COLS, SLOTS = 8, 8, 8, 512, 128
WIDE = COLS + 128
FAR_FIRST = tuple(sorted(range(1, 16), key=lambda k: -min(k, 16 - k)))
STEPS = ((0, 0), (0, -1), (0, 1), (-1, 0), (1, 0))
OFFSETS = tuple((dy, dx) for dy in range(-2, 3) for dx in range(-2, 3) if abs(dy) + abs(dx) <= 2)
N_OFF = len(OFFSETS)
PLANES = 24


def iota(shape, dim):
    return lax.broadcasted_iota(jnp.int32, shape, dim)


def lroll(x, by):
    by = by % x.shape[-1]
    return x if by == 0 else pltpu.roll(x, by, x.ndim - 1)


def rshift(own, halo, by):
    if by == 0:
        return own, halo
    axis = own.ndim - 2
    turned_own = pltpu.roll(own, by % ROWS, axis)
    turned_halo = pltpu.roll(halo, by % ROWS, axis)
    sub = iota(own.shape, axis)
    cross = sub < by if by > 0 else sub >= ROWS + by
    return jnp.where(cross, turned_halo, turned_own), jnp.where(cross, turned_own, turned_halo)


def exact_dot(values, onehot, dims):
    high = values.astype(BF16)
    rest = values - high.astype(F32)
    middle = rest.astype(BF16)
    low = (rest - middle.astype(F32)).astype(BF16)
    dot = lambda part: lax.dot_general(part, onehot, (dims, ((), ())), preferred_element_type=F32)
    return dot(high) + (dot(middle) + dot(low))


def remote(src, dst, send, recv, device):
    return pltpu.make_async_remote_copy(
        src_ref=src, dst_ref=dst, send_sem=send, recv_sem=recv, device_id=device, device_id_type=MESH
    )


def main_kernel(
    all_cells,
    flux_h, prof_h, cour_h, wind_h, cells_h, kern_h, month_h, observed_h, obs_w_h, prec_h, counts,
    fg_out, pg_out,
    prof, cells, kern, month, observed, obs_w, prec, prec_v,
    flux_v, cour_v, wind_v, w_own, w_halo, row_s, row_r, col_s, col_r,
    s_buf, i_buf, z_buf, r_buf, h_buf, f_buf,
    l_buf, slot_v, nb, corner_s, corner_r, dense, m_sh, a_sh, az, ap,
    loc_sem, coef_s, coef_r, st1_s, st1_r, st2_s, st2_r, hal_s, hal_r, fx_s, fx_r,
    lev_s, lev_r, nb_s, nb_r, corner_ss, corner_sr, az_s, az_r, ap_s, ap_r,
):
    face, tile, lev = lax.axis_index("face"), lax.axis_index("tile"), lax.axis_index("lev")
    ty, tz, tx = tile // 16, (tile // 4) % 4, tile % 4
    z, plane = tz * 4 + face, ty * 4 + tx

    def in_plane(k):
        other = lax.rem(plane + k, 16)
        return other, (face, (other // 4) * 16 + tz * 4 + other % 4, lev)

    def in_line(k):
        other = lax.rem(z + k, 16)
        return (other % 4, ty * 16 + (other // 4) * 4 + tx, lev)

    def near(df, dt, core=lev):
        return (lax.rem(face + 4 + df, 4), lax.rem(tile + 64 + dt, 64), core)

    peer = (face, tile, 1 - lev)
    sends = ((0, -1), (0, 1), (-1, 0), (1, 0), (-1, -1), (1, -1), (-1, 1), (1, 1))

    bar = pltpu.get_barrier_semaphore()
    greet = [near(*d, core) for d in sends[4:] for core in (lev, 1 - lev)]
    greet += [in_line(k) for k in FAR_FIRST] + [near(*d) for d in sends[:2]]
    greet += [in_plane(k)[1] for k in range(1, 16)] + [peer]
    for device in greet:
        pl.semaphore_signal(bar, inc=1, device_id=device, device_id_type=MESH)

    local = [
        pltpu.make_async_copy(src, dst, loc_sem.at[i])
        for i, (src, dst) in enumerate(
            (
                (flux_h, flux_v), (cour_h, cour_v), (wind_h, wind_v), (cells_h, cells), (kern_h, kern),
                (prof_h, prof), (obs_w_h, obs_w), (observed_h, observed), (month_h, month), (prec_h, prec), (prec_h, prec_v),
            )
        )
    ]
    for copy in local:
        copy.start()

    local[0].wait()
    by_tracer = jnp.swapaxes(flux_v[...], 0, 1).reshape(NT * 8, 512)
    turned = jnp.transpose(jnp.concatenate([by_tracer, by_tracer], axis=0)).reshape(64, 8, 128)
    nothing = jnp.zeros((1, 8, 128), F32)
    above = jnp.concatenate([turned[1:], nothing], axis=0)
    below = jnp.concatenate([nothing, turned[:-1]], axis=0)
    around = jnp.where(iota((64, 8, 128), 1) < 4, above, below)
    half = jnp.where(lev == 0, turned, around).reshape(4, 2, 2, 4, 8, 128)
    blocks = jnp.where(iota((4, 2, 4, 8, 128), 4) < 64, half[:, :, 0], half[:, :, 1])
    for y in range(4):
        for x in range(4):
            s_buf[y * 4 + x] = blocks[y, :, x]

    local[1].wait()
    local[2].wait()
    u, v = cour_v[0], cour_v[1]
    east, north = wind_v[0] == 1, wind_v[1] == 1
    w_own[1, :, :, :COLS] = jnp.where(east, 0.0, u) + KAPPA
    w_own[2, :, :, :COLS] = jnp.where(east, u, 0.0) + KAPPA
    w_own[3, :, :, :COLS] = jnp.where(north, 0.0, v) + KAPPA
    w_own[4, :, :, :COLS] = jnp.where(north, v, 0.0) + KAPPA
    w_own[0, :, :, :COLS] = 1.0 - u - v - 4.0 * KAPPA
    lane = iota((ROWS, 128), 1)
    last, first = jnp.zeros((ROWS, 128), F32), jnp.zeros((ROWS, 128), F32)
    for e in range(4):
        for l in range(NLEV):
            k = e * NLEV + l
            last = jnp.where(lane == k, lroll(w_own[1 + e, l, :, COLS - 128 : COLS], k - 127), last)
            first = jnp.where(lane == k, lroll(w_own[1 + e, l, :, :128], k), first)
    col_s[0] = last
    col_s[1] = first
    for e in range(4):
        row_s[0, e] = w_own[1 + e, :, ROWS - 1, :COLS]
        row_s[1, e] = w_own[1 + e, :, 0, :COLS]

    pl.semaphore_wait(bar, len(greet))

    coef = [
        remote(row_s.at[0], row_r.at[0], coef_s.at[0], coef_r.at[0], near(0, 1)),
        remote(row_s.at[1], row_r.at[1], coef_s.at[1], coef_r.at[1], near(0, -1)),
        remote(col_s.at[0], col_r.at[0], coef_s.at[2], coef_r.at[2], near(1, 0)),
        remote(col_s.at[1], col_r.at[1], coef_s.at[3], coef_r.at[3], near(-1, 0)),
    ]
    for copy in coef:
        copy.start()
    stage1 = []
    for k in range(1, 16):
        other, device = in_plane(k)
        copy = remote(s_buf.at[other], i_buf.at[plane], st1_s.at[k], st1_r.at[k], device)
        copy.start()
        stage1.append(copy)
    i_buf[plane] = s_buf[plane]

    for copy in local[3:]:
        copy.wait()
    slot = iota((1, SLOTS), 1)
    cell = cells[0].astype(F32)
    row = jnp.floor(cell * (1.0 / COLS))
    col = cell - COLS * row
    sub = iota((ROWS, SLOTS), 0).astype(F32)
    row_mask = jnp.where(sub == row, 1.0, 0.0)
    onehot = jnp.where(iota((COLS, SLOTS), 0).astype(F32) == col, 1.0, 0.0).astype(BF16)
    weight = jnp.where(slot < counts[...], obs_w[0], 0.0)
    kern_rows = (kern[:, 0, 0, :][:, None, :] * row_mask[None]).reshape(NLEV * ROWS, SLOTS)
    kern_dense = exact_dot(kern_rows, onehot, ((1,), (1,))).reshape(NLEV, ROWS, COLS)
    level = iota((NLEV, ROWS, COLS), 0)
    prof_dense = jnp.zeros((NLEV, ROWS, COLS), F32)
    for l in range(NLEV):
        prof_dense = jnp.where(level == l, prof[l], prof_dense)
    kp = kern_dense * prof_dense

    for copy in stage1:
        copy.wait()
    lane6 = iota((2, 4, 8, 128), 3)
    for hi in range(2):
        low_y, high_y = i_buf_view(i_buf, hi)
        z_buf[2 * hi] = jnp.where(lane6 < 64, low_y, lroll(high_y, 64))
        z_buf[2 * hi + 1] = jnp.where(lane6 < 64, lroll(low_y, 64), high_y)
    stage2 = []
    for k in range(1, 4):
        to = lax.rem(tz + k, 4)
        copy = remote(z_buf.at[to], r_buf.at[tz], st2_s.at[k], st2_r.at[k], (face, ty * 16 + to * 4 + tx, lev))
        copy.start()
        stage2.append(copy)

    def halo_copy(side, to):
        there = lax.rem(face + (3 if side == 0 else 1), 4)
        src = (0, 0) if side == 0 else (1, 3)
        device = (there, ty * 16 + to * 4 + tx, lev)
        return remote(z_buf.at[(to, *src)], h_buf.at[side], hal_s.at[side, to], hal_r.at[side], device)

    @pl.when(tz == 0)
    def _():
        for to in range(4):
            halo_copy(0, to).start()

    @pl.when(tz == 3)
    def _():
        for to in range(4):
            halo_copy(1, to).start()

    r_buf[tz] = z_buf[tz]

    for copy in coef:
        copy.wait()
    right, left = col_r[1], col_r[0]
    for e in range(4):
        for l in range(NLEV):
            k = e * NLEV + l
            w_own[1 + e, l, :, COLS:] = jnp.where(
                lane == 0, lroll(right, -k), jnp.where(lane == 127, lroll(left, 127 - k), 0.0)
            )
    w_own[0, :, :, COLS:] = 1.0 - (
        w_own[1, :, :, COLS:] + w_own[2, :, :, COLS:] + w_own[3, :, :, COLS:] + w_own[4, :, :, COLS:]
    )
    sub2 = iota((ROWS, COLS), 0)
    is_up, is_down = (sub2 == 0) & (tile < 63), (sub2 == ROWS - 1) & (tile > 0)
    for l in range(NLEV):
        rest = jnp.where(is_up | is_down, 1.0, 0.0)
        for e in range(4):
            edge = jnp.where(is_up, row_r[1, e, l : l + 1], jnp.where(is_down, row_r[0, e, l : l + 1], 0.0))
            w_halo[1 + e, l] = edge
            rest = rest - edge
        w_halo[0, l] = rest

    stencil = {}

    def add(offset, term):
        stencil[offset] = stencil[offset] + term if offset in stencil else term

    for e1, (dy, dx) in enumerate(STEPS):
        g = kp * w_own[e1, :, :, :COLS]
        for e2, (ey, ex) in enumerate(STEPS):
            offset = (dy + ey, dx + ex)
            if dy == 0 and dx == 0:
                add(offset, jnp.sum(g * w_own[e2, :, :, :COLS], axis=0))
            elif dy == 0:
                h = lroll(jnp.concatenate([g, jnp.zeros((NLEV, ROWS, 128), F32)], axis=-1), dx)
                add(offset, lroll(jnp.sum(h * w_own[e2], axis=0), -dx)[:, :COLS])
            else:
                h, h_halo = rshift(g, jnp.zeros_like(g), dy)
                p, p_halo = jnp.sum(h * w_own[e2, :, :, :COLS], axis=0), jnp.sum(h_halo * w_halo[e2], axis=0)
                add(offset, rshift(p, p_halo, -dy)[0])
    spread = jnp.concatenate([stencil[o] for o in OFFSETS] + [jnp.zeros((3 * ROWS, COLS), F32)], axis=0)
    picked = exact_dot(spread, onehot, ((1,), (0,))).reshape(16, ROWS, SLOTS)
    l_buf[0] = jnp.sum(picked * row_mask[None], axis=1)
    to_peer = remote(l_buf.at[0], l_buf.at[1], lev_s, lev_r, peer)
    to_peer.start()

    sub16 = iota((16, SLOTS), 0)
    core0 = lev == 0
    part = jnp.where(sub16 == 13, jnp.where(core0, observed[0], 0.0), l_buf[0])
    part = jnp.where(sub16 == 14, jnp.where(core0, weight, 0.0), part)
    every = jnp.concatenate([jnp.where(core0, month[:, 0, 0, :], 0.0), part], axis=0)
    lane24, sub24 = iota((PLANES, SLOTS), 1), iota((PLANES, SLOTS), 0)
    corner_copies = []
    for k, corner in enumerate((0.0, COLS - 1.0, (ROWS - 1.0) * COLS, ROWS * COLS - 1.0)):
        found = jnp.sum(jnp.where(cell == corner, every, 0.0), axis=1, keepdims=True)
        line = jnp.sum(jnp.where(lane24 == sub24 + 32 * k, found, 0.0), axis=0, keepdims=True)
        corner_s[k] = jnp.broadcast_to(line, (8, SLOTS))
        for i, core in enumerate((lev, 1 - lev)):
            src, dst = corner_s.at[k, pl.ds(0, 1)], corner_r.at[2 * k + lev, pl.ds(0, 1)]
            copy = remote(src, dst, corner_ss.at[2 * k + i], corner_sr.at[2 * k + lev], near(*sends[4 + k], core))
            copy.start()
            corner_copies.append(copy)
    to_peer.wait()

    table = l_buf[0] + l_buf[1]
    table = jnp.where(sub16 == 13, observed[0], table)
    table = jnp.where(sub16 == 14, weight, table)
    slot_v[8:24] = jnp.where(sub16 == 15, cell, table)
    slot_v[0:8] = month[:, 0, 0, :]
    around_copies = []
    for k, d in enumerate(sends[:4]):
        copy = remote(slot_v, nb.at[k], nb_s.at[k], nb_r.at[k], near(*d))
        copy.start()
        around_copies.append(copy)

    def rows_of(values, mask):
        return (values[:, None, :] * mask[None]).reshape(PLANES * ROWS, SLOTS)

    own = exact_dot(rows_of(slot_v[...], row_mask), onehot, ((1,), (1,)))
    dense[0, :, :, :COLS] = own.reshape(PLANES, ROWS, COLS)

    for copy in stage2:
        copy.wait()

    @pl.when(tz == 0)
    def _():
        for to in range(4):
            halo_copy(0, to).wait_send()

    @pl.when(tz == 3)
    def _():
        for to in range(4):
            halo_copy(1, to).wait_send()

    for side in range(2):
        halo_copy(side, 0).wait_recv()
    parts = [r_buf[i // 4, :, i % 4] for i in range(16)]
    lanes = iota((2, 8, 128), 2)
    for step in (1, 2, 4, 8):
        upper_half = (lanes // (8 * step)) % 2 == 1
        for i in range(16):
            if i & step == 0:
                a, b = parts[i], parts[i + step]
                parts[i] = jnp.where(upper_half, lroll(b, 8 * step), a)
                parts[i + step] = jnp.where(upper_half, b, lroll(a, -8 * step))
    for g in range(16):
        for y in range(2):
            f_buf[lev, g % 8, :, (2 * y + g // 8) * 128 : (2 * y + g // 8 + 1) * 128] = parts[g][y]
    for t in range(NT):
        f_buf[lev, t, :, COLS:] = jnp.where(
            lane < 4, lroll(h_buf[0], -8 * t), jnp.where(lane >= 124, lroll(h_buf[1], 56 - 8 * t), 0.0)
        )
    swap = remote(f_buf.at[lev], f_buf.at[lev], fx_s, fx_r, peer)
    swap.start()

    for copy in around_copies:
        copy.wait()
    for copy in corner_copies:
        copy.wait_send()
    for i in range(8):
        row = corner_r.at[i, pl.ds(0, 1)]
        remote(row, row, corner_ss.at[i], corner_sr.at[i], near(*sends[4 + i // 2])).wait_recv()
    up, down = tile < 63, tile > 0

    def place(k):
        c = nb[k, 23:24, :]
        r = jnp.floor(c * (1.0 / COLS))
        return r, c - COLS * r

    def near_rows(r, upper):
        keep = (r <= 1.0) & up if upper else (r >= 6.0) & down
        return jnp.where((sub == r) & keep, 1.0, 0.0)

    def near_cols(c, righter):
        target = iota((128, SLOTS), 0).astype(F32)
        hit = (target == c) & (c <= 1.0) if righter else (target == c - (COLS - 128.0)) & (c >= COLS - 2.0)
        return jnp.where(hit, 1.0, 0.0).astype(BF16)

    values, hots = [], []
    for k, upper in ((0, True), (1, False)):
        r, c = place(k)
        values.append(rows_of(nb[k], near_rows(r, upper)))
        hots.append(jnp.where(iota((COLS, SLOTS), 0).astype(F32) == c, 1.0, 0.0).astype(BF16))
    out = exact_dot(jnp.concatenate(values, axis=1), jnp.concatenate(hots, axis=1), ((1,), (1,)))
    dense[1, :, :, :COLS] = out.reshape(PLANES, ROWS, COLS)
    values, hots = [], []
    for k, righter in ((2, True), (3, False)):
        r, c = place(k)
        values.append(rows_of(nb[k], jnp.where(sub == r, 1.0, 0.0)))
        hots.append(near_cols(c, righter))
    out = exact_dot(jnp.concatenate(values, axis=1), jnp.concatenate(hots, axis=1), ((1,), (1,)))
    dense[0, :, :, COLS:] = out.reshape(PLANES, ROWS, 128)
    corners = corner_r[0, 0:1]
    for i in range(1, 8):
        corners = corners + corner_r[i, 0:1]
    corners = jnp.where(lane24 % 32 == sub24, corners, 0.0)
    mask = jnp.where(((lane < 64) & (sub == 0.0) & up) | ((lane >= 64) & (sub == ROWS - 1.0) & down), 1.0, 0.0)
    place0, side = iota((128, SLOTS), 0), (iota((128, SLOTS), 1) // 32) % 2
    hot = jnp.where(place0 == 127 * side, 1.0, 0.0).astype(BF16)
    out = exact_dot(rows_of(corners, mask), hot, ((1,), (1,)))
    dense[1, :, :, COLS:] = out.reshape(PLANES, ROWS, 128)

    for dx in range(-2, 3):
        months = lroll(dense[0, 0:8], dx), lroll(dense[1, 0:8], dx)
        for i, (oy, ox) in enumerate(OFFSETS):
            if ox == dx:
                m_own, m_halo = rshift(*months, oy)
                m_sh[i, 0] = m_own
                m_sh[i, 1] = m_halo
                a_own, a_halo = rshift(lroll(dense[0, 8 + i], dx), lroll(dense[1, 8 + i], dx), oy)
                a_sh[i, 0] = a_own
                a_sh[i, 1] = a_halo

    swap.wait()

    by_row = {}
    for i, (dy, dx) in enumerate(OFFSETS):
        pair = tuple(lroll(a_sh[i, h] * jnp.sum(m_sh[i, h] * f_buf[h], axis=0), -dx) for h in range(2))
        by_row[dy] = tuple(p + q for p, q in zip(by_row[dy], pair)) if dy in by_row else pair
    model = None
    for dy, pair in by_row.items():
        pair = rshift(*pair, -dy)
        model = pair if model is None else tuple(p + q for p, q in zip(model, pair))
    forcing = tuple(dense[h, 22] * (dense[h, 21] - model[h]) for h in range(2))
    adj = jnp.zeros((NT, ROWS, COLS), F32)
    for dx in range(-2, 3):
        moved = tuple(lroll(f, dx) for f in forcing)
        for i, (oy, ox) in enumerate(OFFSETS):
            if ox == dx:
                q = (a_sh[i, 0] * rshift(*moved, oy)[0])[:, :COLS]
                adj = adj + q[None] * m_sh[i, 0, :, :, :COLS]

    square = adj * adj
    square = square[..., :128] + square[..., 128:256] + square[..., 256:384] + square[..., 384:]
    square = jnp.sum(square, axis=1)
    for by in (64, 32, 16):
        square = square + lroll(square, by)
    mine = jnp.where(lane // 16 == iota((ROWS, 128), 0), square, 0.0)
    az[z] = jnp.broadcast_to(jnp.sum(mine, axis=0, keepdims=True), (8, 128))
    copies = []
    for k in FAR_FIRST:
        copy = remote(az.at[z, pl.ds(0, 1)], az.at[z, pl.ds(0, 1)], az_s.at[k], az_r.at[k], in_line(k))
        copy.start()
        copies.append(copy)
    for t in range(NT):
        fg_out[t] = prec[t] * f_buf[0, t, :, :COLS] - adj[t]
    for copy in copies:
        copy.wait()
    total = az[0, 0:1]
    for i in range(1, 16):
        total = total + az[i, 0:1]
    ap[plane] = jnp.broadcast_to(total, (8, 128))
    copies = []
    for k in range(1, 16):
        copy = remote(ap.at[plane, pl.ds(0, 1)], ap.at[plane, pl.ds(0, 1)], ap_s.at[k], ap_r.at[k], in_plane(k)[1])
        copy.start()
        copies.append(copy)
    for copy in copies:
        copy.wait()
    total = ap[0, 0:1]
    for i in range(1, 16):
        total = total + ap[i, 0:1]
    sums = jnp.sum(jnp.where(lane // 16 == iota((ROWS, 128), 0), total, 0.0), axis=1, keepdims=True)
    sums = jnp.sum(jnp.where(lane == iota((ROWS, 128), 0), sums, 0.0), axis=0, keepdims=True)[:, :NT]
    p = prec_v[...].reshape(1, NT)
    pg_out[...] = (0.5 / p - 0.5 * (sums / all_cells) / (p * p)).reshape(NT)


def i_buf_view(i_buf, hi):
    low = jnp.concatenate([i_buf[0:4, hi][None], i_buf[8:12, hi][None]], axis=0)
    high = jnp.concatenate([i_buf[4:8, hi][None], i_buf[12:16, hi][None]], axis=0)
    return low, high


def on_device(flux, profile, courant, winds, cells, counts, kernels, month_weight, observed, obs_weight, precision):
    vmem = pl.BlockSpec(memory_space=pltpu.VMEM)
    hbm = pl.BlockSpec(memory_space=pltpu.HBM)
    dma = pltpu.SemaphoreType.DMA

    def buf(*shape, dtype=F32):
        return pltpu.VMEM(shape, dtype)

    def smem(*shape, dtype=F32):
        return pltpu.SMEM(shape, dtype)

    all_cells = float(ROWS * COLS * lax.axis_size("tile") * lax.axis_size("face"))
    return pl.pallas_call(
        functools.partial(main_kernel, all_cells),
        name="gradient",
        out_shape=(jax.ShapeDtypeStruct((NT, ROWS, COLS), F32), jax.ShapeDtypeStruct((NT,), F32)),
        in_specs=[hbm] * 10 + [vmem],
        out_specs=(vmem, vmem),
        scratch_shapes=[
            smem(NLEV), buf(1, 1, SLOTS, dtype=jnp.int32), buf(NLEV, 1, 1, SLOTS), buf(NT, 1, 1, SLOTS),
            buf(1, 1, SLOTS), buf(1, 1, SLOTS), smem(NT), buf(NT),
            buf(8, NT, 512), buf(2, NLEV, ROWS, COLS), buf(2, NLEV, ROWS, COLS, dtype=jnp.int32),
            buf(5, NLEV, ROWS, WIDE), buf(5, NLEV, ROWS, COLS), buf(2, 4, NLEV, COLS), buf(2, 4, NLEV, COLS),
            buf(2, 8, 128), buf(2, 8, 128),
            buf(16, 2, 8, 128), buf(16, 2, 8, 128), buf(4, 2, 4, 8, 128), buf(4, 2, 4, 8, 128), buf(2, 8, 128),
            buf(2, NT, ROWS, WIDE),
            buf(2, 16, SLOTS), buf(PLANES, SLOTS), buf(4, PLANES, SLOTS), buf(4, 8, SLOTS), buf(8, 8, SLOTS),
            buf(2, PLANES, ROWS, WIDE),
            buf(N_OFF, 2, NT, ROWS, WIDE), buf(N_OFF, 2, ROWS, WIDE), buf(16, 8, 128), buf(16, 8, 128),
            dma((11,)), dma((4,)), dma((4,)), dma((16,)), dma((16,)), dma((4,)), dma((4,)), dma((2, 4)), dma((2,)), dma, dma,
            dma, dma, dma((4,)), dma((4,)), dma((8,)), dma((8,)), dma((16,)), dma((16,)), dma((16,)), dma((16,)),
        ],
        compiler_params=pltpu.CompilerParams(collective_id=0, has_side_effects=True, vmem_limit_bytes=40 * 2**20),
    )(
        *(
            pltpu.with_memory_space_constraint(x, pltpu.HBM)
            for x in (flux, profile, courant, winds, cells, kernels, month_weight, observed, obs_weight, precision)
        ),
        jnp.broadcast_to(counts, (1, SLOTS)),
    )


def solution(mesh):
    return jax.shard_map(
        on_device,
        mesh=mesh,
        in_specs=(
            P(("face", "tile"), None, None),
            P("lev"),
            P(None, "lev", "tile", "face"),
            P(None, "lev", "tile", "face"),
            P("tile", "face", None),
            P("tile", "face"),
            P("lev", "tile", "face", None),
            P(None, "tile", "face", None),
            P("tile", "face", None),
            P("tile", "face", None),
            P(),
        ),
        out_specs=(P(None, "tile", "face"), P()),
        check_vma=False,
    )
```
